128 devices in a mesh: rep: 8 (over x, core), head: 4 (over y), side: 4 (over z).
Axes of the slice: x: 4, y: 4, z: 4, core: 2. Of those that a mesh axis runs over, the one named last changes fastest.
Arguments:
- tokens: bfloat16 [8192, 7168], P(('rep', 'head', 'side')), may hold values from -6 to 6
- routes: int32 [8192, 2], P(('rep', 'head', 'side')), may hold values from 0 to 31, all different within a row; in each aligned block of 64 rows (0 to 63, 64 to 127, ...) at most 8 rows name the same one
- gates: float32 [8192, 2], P(('rep', 'head', 'side')), may hold values from 0.2 to 1.5
- w_gate: bfloat16 [32, 7168, 2048], P(('rep', 'head'), None, 'side'), may hold values from -0.0625 to 0.0625
- w_up: bfloat16 [32, 7168, 2048], P(('rep', 'head'), None, 'side'), may hold values from -0.0625 to 0.0625
- w_down: bfloat16 [32, 2048, 7168], P(('rep', 'head'), 'side'), may hold values from -0.125 to 0.125
Outputs:
- moe_out: bfloat16 [8192, 7168], P(('rep', 'head', 'side'))
The draws below stay inside these ranges and needn't reach their ends.
Inputs may be any that keep to these rules, and one draw needn't show every extreme that they name: `routes`: within the rows of one device no expert is named more than 8 times, and in every draw some device names some expert exactly 8 times; a token's 2 experts differ.
All inputs are finite; a program needn't handle non-finite values.
Results may differ from the reference program's by a relative error of at most 0.017.
Values may be sent and summed in bfloat16 or wider, within the bound.
A program may use at most 128 MiB of HBM per device.

```python
import math
import jax
import jax.numpy as jnp
import numpy as np
from jax import lax

D = 7168
FF = 2048
TOP = 2
TOK_DEV = 64
TOKENS = 8192
EXPERTS = 32
CAP = 8
HID_DEV = 512
N_REP = 8
N_HEAD = 4
N_SIDE = 4


def block_scale(rng, dims, pieces, low, largest):
    level, own = 1.0, jax.random.fold_in(rng, 6)
    for dim, parts in pieces:
        steps = jnp.exp(jax.random.uniform(jax.random.fold_in(own, dim), (parts,), jnp.float32, low / len(pieces), largest / len(pieces)))
        level = level * jnp.repeat(steps, dims[dim] // parts).reshape([-1 if axis == dim else 1 for axis in range(len(dims))])
    return level


def routed_block(stream_key, own, number, rows, number_of, top, most, slope):
    sequence = jax.random.permutation(stream_key, number_of)
    packed, usual = load_shares(number_of, rows * top, most, slope, True), load_shares(number_of, rows * top, most, slope, False)
    places = jnp.arange(number_of)

    def named(tallies, turn):
        used = int((tallies > 0).sum())
        fixed = max(1, used // 4)
        shifted = fixed + (places - fixed + turn * (used - fixed)) % max(1, number_of - fixed)
        return jnp.zeros((number_of,), jnp.int32).at[sequence[jnp.where(places < fixed, places, shifted)]].set(jnp.asarray(tallies, jnp.int32))

    tallies = jnp.where(number % 4 == 0, named(packed, number // 4), named(usual, number - number // 4 - 1))
    mixed = jax.random.permutation(jax.random.fold_in(own, 3), number_of)
    donor, taker = mixed[0:number_of // 2 * 2:2], mixed[1:number_of // 2 * 2:2]
    slack = jnp.minimum(tallies[donor] - 1, most - tallies[taker]) // 2
    slack = jnp.where((donor == sequence[0]) | (taker == sequence[0]) | (tallies[taker] == 0), 0, jnp.maximum(slack, 0))
    shifted = jax.random.randint(jax.random.fold_in(own, 4), (number_of // 2,), 0, 1 << 20) % (slack + 1)
    tallies = tallies.at[donor].add(-shifted).at[taker].add(shifted)
    items = jnp.searchsorted(jnp.cumsum(tallies), jnp.arange(rows * top), side="right").astype(jnp.int32)
    listing = items.reshape(top, rows).T
    listing = listing[jax.random.permutation(jax.random.fold_in(own, 1), rows)]
    turn = jax.random.randint(jax.random.fold_in(own, 2), (rows, 1), 0, top)
    return jnp.take_along_axis(listing, (jnp.arange(top)[None, :] + turn) % top, axis=1)


def load_shares(number_of, total, bound, slope, full):
    loads = [(1 << 20) // math.isqrt(standing ** slope) + 1 for standing in range(1, number_of + 1)]
    largest = bound if full else min(bound, max(-(-total // number_of), total * loads[0] // sum(loads)))
    least = 1 if total - largest >= number_of - 1 else 0
    counts, surplus = [largest] + [least] * (number_of - 1), total - largest - least * (number_of - 1)
    while surplus > 0:
        movable = [i for i in range(1, number_of) if counts[i] < largest] or [i for i in range(1, number_of) if counts[i] < bound]
        mass, remaining = sum([loads[i] for i in movable]), surplus
        for i in movable:
            extra = min(bound - counts[i], max(1, remaining * loads[i] // mass), surplus)
            counts[i] = counts[i] + extra
            surplus = surplus - extra
    return np.array(counts)


def gaussian(own_key, dims, deviation, reach, pieces=(), dtype=jnp.bfloat16):
    result = jax.random.normal(own_key, dims, jnp.float32) * deviation
    if len(pieces) > 0:
        result = block_scale(own_key, dims, pieces, -0.22, 0.18) * result
    return jnp.clip(result, min=-reach, max=reach).astype(dtype)


def setup_inputs(seed: int = 0) -> dict:
    arg_keys = jax.random.split(jax.random.key(seed), 7)
    tokens = gaussian(arg_keys[0], (TOKENS, D), 1.0, 6.0, ((0, 128),))
    routes_keys = jax.random.split(jax.random.fold_in(arg_keys[1], 1), TOKENS // TOK_DEV)
    routes_turns = jax.random.permutation(jax.random.fold_in(arg_keys[1], 3), TOKENS // TOK_DEV)
    routes = jax.vmap(lambda own, number: routed_block(jax.random.fold_in(arg_keys[1], 2), own, number, TOK_DEV, EXPERTS, TOP, CAP, 2))(routes_keys, routes_turns).reshape((TOKENS, TOP))
    gates = jnp.clip(0.2 + 1.3 * jax.random.uniform(arg_keys[2], (TOKENS, TOP), jnp.float32) ** block_scale(arg_keys[2], (TOKENS, TOP), ((0, 128),), -0.2, 0.2), 0.2, 1.5)
    w_gate = gaussian(arg_keys[3], (EXPERTS, D, FF), D ** -0.5, 0.0625, ((0, 32), (2, 4)))
    w_up = gaussian(arg_keys[4], (EXPERTS, D, FF), D ** -0.5, 0.0625, ((0, 32), (2, 4)))
    w_down = gaussian(arg_keys[5], (EXPERTS, FF, D), FF ** -0.5, 0.125, ((0, 32), (1, 4)))
    return dict(tokens=tokens, routes=routes, gates=gates, w_gate=w_gate, w_up=w_up, w_down=w_down)


def reference(tokens, routes, gates, w_gate, w_up, w_down):
    device_count = N_REP * N_HEAD * N_SIDE
    slices = N_SIDE
    flat_routes = routes.reshape(device_count, TOK_DEV * TOP)
    onehot = (flat_routes[:, :, None] == jnp.arange(EXPERTS)[None, None, :]).astype(jnp.int32)
    before = jnp.cumsum(onehot, axis=1) - onehot
    slot_index = jnp.sum(before * onehot, axis=2)
    target = ((flat_routes * device_count + jnp.arange(device_count)[:, None]) * CAP + slot_index).reshape(-1).astype(jnp.int32)
    token_rows = jnp.repeat(tokens, TOP, axis=0)
    buffer = jnp.zeros((EXPERTS * device_count * CAP, D), jnp.bfloat16).at[target].set(token_rows)
    buffer = buffer.reshape(EXPERTS, device_count * CAP, D)

    def expert_one(items):
        slot_rows, gate_w, up_w, down_w = items
        gate_proj = jnp.dot(slot_rows, gate_w, preferred_element_type=jnp.float32)
        up_proj = jnp.dot(slot_rows, up_w, preferred_element_type=jnp.float32)
        hidden = (jax.nn.silu(gate_proj) * up_proj).astype(jnp.bfloat16)
        blocks = hidden.reshape(slot_rows.shape[0], slices, HID_DEV).astype(jnp.float32)
        down_blocks = down_w.reshape(slices, HID_DEV, D).astype(jnp.float32)
        partial_value = jnp.einsum('rsh,shd->srd', blocks, down_blocks).astype(jnp.bfloat16)
        return jnp.sum(partial_value.astype(jnp.float32), axis=0).astype(jnp.bfloat16)

    expert_out = lax.map(expert_one, (buffer, w_gate, w_up, w_down)).reshape(EXPERTS * device_count * CAP, D)
    picked = expert_out[target].reshape(TOKENS, TOP, D).astype(jnp.float32)
    return jnp.sum(picked * gates[:, :, None], axis=1).astype(jnp.bfloat16)
```

```python
import functools

import jax
import jax.numpy as jnp
from jax import lax
from jax.experimental import pallas as pl
from jax.experimental.pallas import tpu as pltpu
from jax.sharding import PartitionSpec as P

MESH = pl.DeviceIdType.MESH
F32, BF16 = jnp.float32, jnp.bfloat16
CW = 512
K2 = 4
CAP = 8
TOK = 64
NX, NY, NZ = 4, 4, 4
PLANE = NX * NY
OFFS = [(dx, dy) for dx in range(NX) for dy in range(NY) if (dx, dy) != (0, 0)]


class Place:
    def __init__(self):
        rep = lax.axis_index("rep")
        self.x, self.c = rep // 2, rep % 2
        self.y, self.z = lax.axis_index("head"), lax.axis_index("side")
        self.j = self.x * NY + self.y
        self.up, self.down = lax.rem(self.z + 1, NZ), lax.rem(self.z + NZ - 1, NZ)
        self.core = self.dev(self.x, 1 - self.c, self.y, self.z)
        self.z_up = self.dev(self.x, self.c, self.y, self.up)
        self.z_down = self.dev(self.x, self.c, self.y, self.down)

    def dev(self, x, c, y, z):
        return (x * 2 + c, y, z)

    def plane(self, off):
        x, y = lax.rem(self.x + off[0], NX), lax.rem(self.y + off[1], NY)
        return x * NY + y, self.dev(x, self.c, y, self.z)

    def column(self):
        own = []
        for dc in range(2):
            for dz in range(NZ):
                if (dc, dz) != (0, 0):
                    own.append(self.dev(self.x, lax.rem(self.c + dc, 2), self.y, lax.rem(self.z + dz, NZ)))
        return own


def enter(partners):
    barrier = pltpu.get_barrier_semaphore()
    for device in partners:
        pl.semaphore_signal(barrier, inc=1, device_id=device, device_id_type=MESH)
    pl.semaphore_wait(barrier, len(partners))


def send(src, dst, send_sem, recv_sem, device):
    pltpu.make_async_remote_copy(
        src_ref=src, dst_ref=dst, send_sem=send_sem, recv_sem=recv_sem, device_id=device, device_id_type=MESH
    ).start()


def done(ref, sem):
    pltpu.make_async_copy(ref, ref, sem).wait()


def dispatch_kernel(
    k1, tok, meta, wg_hbm, wu_hbm, hid, gpk,
    tokc, ztok, metas, pk, out1, out2, x1, x2, wg, wu, acc,
    w_sem, m_send, m_recv, c_send, c_recv, t_send, t_recv, tc_send, tc_recv,
    a1_send, a1_recv, z_send, z_recv, f_send, f_recv, a2_send, a2_recv,
):
    me = Place()
    d1 = k1 * CW
    half = TOK // 2
    for kk in range(k1 + K2):
        rows = pl.ds(kk * CW, CW)
        pltpu.make_async_copy(wg_hbm.at[rows], wg.at[rows], w_sem.at[0, kk]).start()
        pltpu.make_async_copy(wu_hbm.at[rows], wu.at[rows], w_sem.at[1, kk]).start()
    enter([me.plane(off)[1] for off in OFFS] + me.column())

    own_meta = metas.at[me.z, me.c]
    pltpu.make_async_copy(meta, own_meta, m_recv).start()
    for i, device in enumerate(me.column()):
        send(meta, own_meta, m_send.at[i], m_recv, device)
    core_rows = pl.ds(pl.multiple_of(me.c * TOK, TOK), TOK)
    for k in range(k1):
        cols = pl.ds(k * CW, CW)
        pltpu.make_async_copy(tok.at[:, cols], tokc.at[k, core_rows], c_recv.at[k]).start()
        send(tok.at[:, cols], tokc.at[k, core_rows], c_send.at[k], c_recv.at[k], me.core)
    tail = pl.ds(d1, K2 * CW)
    own_tok = ztok.at[me.z, core_rows]
    pltpu.make_async_copy(tok.at[:, tail], own_tok, t_recv.at[4]).start()
    send(tok.at[:, tail], own_tok, t_send.at[0], t_recv.at[0], me.z_up)
    send(tok.at[:, tail], own_tok, t_send.at[1], t_recv.at[1], me.z_down)

    done(metas, m_recv)
    shape = (2 * PLANE * CAP, 2 * TOK)
    row = lax.broadcasted_iota(jnp.int32, shape, 0)
    col = lax.broadcasted_iota(jnp.int32, shape, 1)
    dest = row // (2 * CAP)
    want = ((2 * (dest // NY) + me.c) * NY + dest % NY) * CAP + row % CAP
    want = jnp.where((row // CAP) % 2 == col // TOK, want, -1).astype(F32)
    for zz in range(NZ):
        both = metas[zz, 0] + metas[zz, 1]
        hit0, hit1 = want == both[0:1], want == both[1:2]
        pk[zz] = jnp.where(hit0 | hit1, 1.0, 0.0).astype(BF16)
        gated = jnp.where(hit0, both[2:3], 0.0) + jnp.where(hit1, both[3:4], 0.0)
        gated = gated.T
        high = gated.astype(BF16)
        gpk[zz, 0] = high
        gpk[zz, 1] = (gated - high.astype(F32)).astype(BF16)

    def p1_issue(k):
        done(tokc.at[k], c_recv.at[k])
        picked = jnp.dot(pk[me.z], tokc[k], preferred_element_type=F32)
        out1[k] = picked.astype(BF16).reshape(PLANE, 2 * CAP, CW)
        here = x1.at[k, me.z, me.j]
        for off in OFFS:
            j, device = me.plane(off)
            send(out1.at[k, j], here, a1_send.at[k], a1_recv.at[k], device)
        pltpu.make_async_copy(out1.at[k, me.j], here, a1_recv.at[k]).start()

    def z_issue(k):
        block = x1.at[k, me.z]
        done(block, a1_recv.at[k])
        send(block, block, z_send.at[k, 0], z_recv.at[k, 0], me.z_up)
        send(block, block, z_send.at[k, 1], z_recv.at[k, 1], me.z_down)

    def z_forward(k):
        low, high = pl.ds(0, PLANE // 2), pl.ds(PLANE // 2, PLANE // 2)
        done(x1.at[k, me.down], z_recv.at[k, 0])
        part = x1.at[k, me.down, low]
        send(part, part, f_send.at[k, 0], f_recv.at[k, 0], me.z_up)
        done(x1.at[k, me.up], z_recv.at[k, 1])
        part = x1.at[k, me.up, high]
        send(part, part, f_send.at[k, 1], f_recv.at[k, 1], me.z_down)

    def project(block, kk):
        rows = pl.ds(pl.multiple_of(kk * CW, CW), CW)
        done(wg.at[rows], w_sem.at[0, kk])
        done(wu.at[rows], w_sem.at[1, kk])
        hid_cols = wg.shape[1]
        for base, w in ((0, wg), (hid_cols, wu)):
            @pl.loop(0, hid_cols // 256)
            def _(n):
                cols = pl.ds(pl.multiple_of(n * 256, 256), 256)
                to = pl.ds(pl.multiple_of(base + n * 256, 256), 256)
                part = jnp.dot(block[...].reshape(acc.shape[0], CW), w[rows, cols], preferred_element_type=F32)
                acc[:, to] = acc[:, to] + part

    def mm1(k):
        across = lax.rem(me.z + 2, NZ)
        done(x1.at[k, across, pl.ds(0, PLANE // 2)], f_recv.at[k, 0])
        done(x1.at[k, across, pl.ds(PLANE // 2, PLANE // 2)], f_recv.at[k, 1])
        project(x1.at[k], k)

    def p2_issue(m):
        cols = pl.ds(pl.multiple_of(m * CW, CW), CW)

        @pl.loop(0, NZ)
        def _(zz):
            picked = jnp.dot(pk[zz], ztok[zz, :, cols], preferred_element_type=F32)
            out2[m, zz] = picked.astype(BF16).reshape(PLANE, 2 * CAP, CW)

        here = x2.at[m, :, me.j]
        for off in OFFS:
            j, device = me.plane(off)
            send(out2.at[m, :, j], here, a2_send.at[m], a2_recv.at[m], device)
        pltpu.make_async_copy(out2.at[m, :, me.j], here, a2_recv.at[m]).start()

    def mm2(m):
        done(x2.at[m], a2_recv.at[m])
        project(x2.at[m], k1 + m)

    p1_issue(0)
    p1_issue(1)
    done(ztok.at[me.down, core_rows], t_recv.at[0])
    part = ztok.at[me.down, pl.ds(pl.multiple_of(me.c * TOK, TOK), half)]
    send(part, part, t_send.at[2], t_recv.at[2], me.z_up)
    done(ztok.at[me.up, core_rows], t_recv.at[1])
    part = ztok.at[me.up, pl.ds(pl.multiple_of(me.c * TOK + half, half), half)]
    send(part, part, t_send.at[3], t_recv.at[3], me.z_down)
    z_issue(0)
    p1_issue(2)
    acc[...] = jnp.zeros_like(acc)
    across = lax.rem(me.z + 2, NZ)
    done(ztok.at[across, pl.ds(pl.multiple_of(me.c * TOK, TOK), half)], t_recv.at[2])
    done(ztok.at[across, pl.ds(pl.multiple_of(me.c * TOK + half, half), half)], t_recv.at[3])
    done(own_tok, t_recv.at[4])
    mine = ztok.at[:, core_rows]
    send(mine, mine, tc_send, tc_recv, me.core)
    z_issue(1)
    other = ztok.at[:, pl.ds(pl.multiple_of((1 - me.c) * TOK, TOK), TOK)]
    done(other, tc_recv)

    @pl.loop(0, k1 + 2)
    def _(k):
        @pl.when((k % 2 == 0) & (k // 2 < K2))
        def _():
            p2_issue(k // 2)

        @pl.when((k >= 2) & (k < k1))
        def _():
            z_issue(k)

        @pl.when((k >= 1) & (k < k1 + 1))
        def _():
            z_forward(k - 1)

        @pl.when(k + 3 < k1)
        def _():
            p1_issue(k + 3)

        @pl.when(k >= 2)
        def _():
            mm1(k - 2)

        @pl.when((k >= 5) & (k % 2 == 1) & ((k - 5) // 2 < K2))
        def _():
            mm2((k - 5) // 2)

    @pl.loop(0, acc.shape[0] // 128)
    def _(i):
        rows = pl.ds(pl.multiple_of(i * 128, 128), 128)
        hc = wg.shape[1]
        g, u = acc[rows, :hc], acc[rows, hc:]
        hid[rows, :] = (g / (1.0 + jnp.exp(-g)) * u).astype(BF16)

    for i in range(2 * NZ - 1):
        done(meta, m_send.at[i])
    done(tok.at[:, tail], t_send.at[0])
    done(tok.at[:, tail], t_send.at[1])
    done(ztok.at[0, pl.ds(0, half)], t_send.at[2])
    done(ztok.at[0, pl.ds(0, half)], t_send.at[3])
    done(mine, tc_send)

    @pl.loop(0, k1)
    def _(k):
        done(tokc.at[k, pl.ds(0, TOK)], c_send.at[k])
        done(out1.at[k, pl.ds(0, PLANE - 1)], a1_send.at[k])
        for side in range(2):
            done(x1.at[k, 0], z_send.at[k, side])
            done(x1.at[k, 0, pl.ds(0, PLANE // 2)], f_send.at[k, side])

    @pl.loop(0, K2)
    def _(m):
        done(out2.at[m, :, pl.ds(0, PLANE - 1)], a2_send.at[m])


def return_kernel(
    k1, hid, gpk, wd_hbm, out,
    wd, y1, y2, s1, s2, r1, l1, l2, t1, e1, t2, e2, u2, v1, v2,
    w_sem, s1_send, s1_recv, s2_send, s2_recv, a1_send, a1_recv, e1_send, e1_recv,
    a2_send, a2_recv, e2_send, e2_recv, v1_send, v1_recv, v2_send, v2_recv,
):
    me = Place()
    half = TOK // 2
    low, high = pl.ds(0, PLANE // 2), pl.ds(PLANE // 2, PLANE // 2)
    across = lax.rem(me.z + 2, NZ)
    own_rows = pl.ds(pl.multiple_of(me.c * TOK, TOK), TOK)
    core_rows = pl.ds(pl.multiple_of((1 - me.c) * TOK, TOK), TOK)
    for kk in range(k1 + K2):
        pltpu.make_async_copy(wd_hbm.at[:, pl.ds(kk * CW, CW)], wd.at[kk], w_sem.at[kk]).start()
    enter([me.plane(off)[1] for off in OFFS] + [me.core, me.z_up, me.z_down])

    def down(to, kk):
        done(wd.at[kk], w_sem.at[kk])

        @pl.loop(0, CW // 256)
        def _(n):
            cols = pl.ds(pl.multiple_of(n * 256, 256), 256)
            part = jnp.dot(hid[...], wd[kk, :, cols], preferred_element_type=F32)
            to[:, :, :, cols] = part.astype(BF16).reshape(NZ, PLANE, 2 * CAP, 256)

    def plus(a, b):
        return (a.astype(F32) + b.astype(F32)).astype(BF16)

    def first(k):
        down(y1.at[k], k)
        send(y1.at[k, across, low], s1.at[k, 0], s1_send.at[k, 0], s1_recv.at[k, 0], me.z_up)
        send(y1.at[k, across, high], s1.at[k, 1], s1_send.at[k, 1], s1_recv.at[k, 1], me.z_down)

    def second(k):
        done(s1.at[k, 0], s1_recv.at[k, 0])
        y1[k, me.up, low] = plus(y1[k, me.up, low], s1[k, 0])
        send(y1.at[k, me.up], s2.at[k, 0], s2_send.at[k, 0], s2_recv.at[k, 0], me.z_up)
        done(s1.at[k, 1], s1_recv.at[k, 1])
        y1[k, me.down, high] = plus(y1[k, me.down, high], s1[k, 1])
        send(y1.at[k, me.down], s2.at[k, 1], s2_send.at[k, 1], s2_recv.at[k, 1], me.z_down)

    def third(k):
        done(s2.at[k, 0], s2_recv.at[k, 0])
        done(s2.at[k, 1], s2_recv.at[k, 1])
        r1[k] = (y1[k, me.z].astype(F32) + s2[k, 0].astype(F32) + s2[k, 1].astype(F32)).astype(BF16)
        here = l1.at[k, me.j]
        for off in OFFS:
            j, device = me.plane(off)
            send(r1.at[k, j], here, a1_send.at[k], a1_recv.at[k], device)
        pltpu.make_async_copy(r1.at[k, me.j], here, a1_recv.at[k]).start()

    def combine(zz, rows):
        rows = rows.reshape(2 * PLANE * CAP, CW)
        return jnp.dot(gpk[zz, 0], rows, preferred_element_type=F32) + jnp.dot(
            gpk[zz, 1], rows, preferred_element_type=F32
        )

    def fourth(k):
        done(l1.at[k], a1_recv.at[k])
        t1[k] = combine(me.z, l1[k])
        send(t1.at[k, core_rows], e1.at[k], e1_send.at[k], e1_recv.at[k], me.core)

    def fifth(k):
        done(e1.at[k], e1_recv.at[k])
        out[:, pl.ds(pl.multiple_of(k * CW, CW), CW)] = (t1[k, own_rows] + e1[k]).astype(BF16)

    def other_first(m):
        down(y2.at[m], k1 + m)
        here = l2.at[m, :, me.j]
        for off in OFFS:
            j, device = me.plane(off)
            send(y2.at[m, :, j], here, a2_send.at[m], a2_recv.at[m], device)
        pltpu.make_async_copy(y2.at[m, :, me.j], here, a2_recv.at[m]).start()

    def other_second(m):
        done(l2.at[m], a2_recv.at[m])

        @pl.loop(0, NZ)
        def _(zz):
            t2[m, zz] = combine(zz, l2[m, zz])

        send(t2.at[m, :, core_rows], e2.at[m], e2_send.at[m], e2_recv.at[m], me.core)

    def other_third(m):
        done(e2.at[m], e2_recv.at[m])
        for zz in range(NZ):
            u2[m, zz] = (t2[m, zz, own_rows] + e2[m, zz]).astype(BF16)
        send(u2.at[m, across, pl.ds(0, half)], v1.at[m, 0], v1_send.at[m, 0], v1_recv.at[m, 0], me.z_up)
        send(u2.at[m, across, pl.ds(half, half)], v1.at[m, 1], v1_send.at[m, 1], v1_recv.at[m, 1], me.z_down)

    def other_fourth(m):
        done(v1.at[m, 0], v1_recv.at[m, 0])
        u2[m, me.up, :half] = plus(u2[m, me.up, :half], v1[m, 0])
        send(u2.at[m, me.up], v2.at[m, 0], v2_send.at[m, 0], v2_recv.at[m, 0], me.z_up)
        done(v1.at[m, 1], v1_recv.at[m, 1])
        u2[m, me.down, half:] = plus(u2[m, me.down, half:], v1[m, 1])
        send(u2.at[m, me.down], v2.at[m, 1], v2_send.at[m, 1], v2_recv.at[m, 1], me.z_down)

    def other_fifth(m):
        done(v2.at[m, 0], v2_recv.at[m, 0])
        done(v2.at[m, 1], v2_recv.at[m, 1])
        total = u2[m, me.z].astype(F32) + v2[m, 0].astype(F32) + v2[m, 1].astype(F32)
        out[:, pl.ds(pl.multiple_of((k1 + m) * CW, CW), CW)] = total.astype(BF16)

    def between(k, lag, count, step):
        @pl.when((k >= lag) & (k < lag + count))
        def _():
            step(k - lag)

    def every_second(k, lag, step):
        @pl.when((k >= lag) & ((k - lag) % 2 == 0) & ((k - lag) // 2 < K2))
        def _():
            step((k - lag) // 2)

    @pl.loop(0, k1 + 5)
    def _(k):
        between(k, 0, k1, first)
        between(k, 0, K2, other_first)
        between(k, 1, k1, second)
        between(k, 2, k1, third)
        between(k, 3, k1, fourth)
        between(k, 4, k1, fifth)
        every_second(k, 3, other_second)
        every_second(k, 4, other_third)
        every_second(k, 5, other_fourth)
        every_second(k, 6, other_fifth)

    @pl.loop(0, k1)
    def _(k):
        for side in range(2):
            done(s1.at[k, 0], s1_send.at[k, side])
            done(s2.at[k, 0], s2_send.at[k, side])
        done(r1.at[k, pl.ds(0, PLANE - 1)], a1_send.at[k])
        done(e1.at[k], e1_send.at[k])

    @pl.loop(0, K2)
    def _(m):
        done(y2.at[m, :, pl.ds(0, PLANE - 1)], a2_send.at[m])
        done(e2.at[m], e2_send.at[m])
        for side in range(2):
            done(v1.at[m, 0], v1_send.at[m, side])
            done(v2.at[m, 0], v2_send.at[m, side])


def on_device(tokens, routes, gates, w_gate, w_up, w_down):
    width = tokens.shape[1]
    k1 = width // CW - K2
    hid_cols = w_gate.shape[2]
    rows = NZ * PLANE * 2 * CAP
    experts = 2 * PLANE
    flat = routes.reshape(-1)
    onehot = (flat[:, None] == jnp.arange(experts)[None, :]).astype(jnp.int32)
    before = jnp.cumsum(onehot, axis=0) - onehot
    slot = jnp.sum(before * onehot, axis=1)
    target = (flat * CAP + slot).reshape(routes.shape).astype(F32)
    meta = jnp.concatenate([target, gates], axis=1).T
    core = lax.axis_index("rep") % 2
    lane_core = lax.broadcasted_iota(jnp.int32, (4, 2 * TOK), 1) // TOK
    meta = jnp.where(lane_core == core, jnp.concatenate([meta, meta], axis=1), 0.0)
    meta = jnp.concatenate([meta, jnp.zeros((4, 2 * TOK), F32)], axis=0)

    dma = pltpu.SemaphoreType.DMA
    vmem = pl.BlockSpec(memory_space=pltpu.VMEM)
    hbm = pl.BlockSpec(memory_space=pl.ANY)
    slots = 2 * CAP
    hid, gpk = pl.pallas_call(
        functools.partial(dispatch_kernel, k1),
        out_shape=(
            jax.ShapeDtypeStruct((rows, hid_cols), BF16),
            jax.ShapeDtypeStruct((NZ, 2, 2 * TOK, PLANE * slots), BF16),
        ),
        in_specs=[vmem, vmem, hbm, hbm],
        out_specs=(vmem, vmem),
        scratch_shapes=[
            pltpu.VMEM((k1, 2 * TOK, CW), BF16),
            pltpu.VMEM((NZ, 2 * TOK, K2 * CW), BF16),
            pltpu.VMEM((NZ, 2, 8, 2 * TOK), F32),
            pltpu.VMEM((NZ, PLANE * slots, 2 * TOK), BF16),
            pltpu.VMEM((k1, PLANE, slots, CW), BF16),
            pltpu.VMEM((K2, NZ, PLANE, slots, CW), BF16),
            pltpu.VMEM((k1, NZ, PLANE, slots, CW), BF16),
            pltpu.VMEM((K2, NZ, PLANE, slots, CW), BF16),
            pltpu.VMEM((width, hid_cols), BF16),
            pltpu.VMEM((width, hid_cols), BF16),
            pltpu.VMEM((rows, 2 * hid_cols), F32),
            dma((2, k1 + K2)), dma((2 * NZ - 1,)), dma, dma((k1,)), dma((k1,)), dma((4,)), dma((5,)), dma, dma,
            dma((k1,)), dma((k1,)), dma((k1, 2)), dma((k1, 2)), dma((k1, 2)), dma((k1, 2)), dma((K2,)), dma((K2,)),
        ],
        compiler_params=pltpu.CompilerParams(collective_id=0, has_side_effects=True, vmem_limit_bytes=60 << 20),
    )(tokens, meta, w_gate[0], w_up[0])

    return pl.pallas_call(
        functools.partial(return_kernel, k1),
        out_shape=jax.ShapeDtypeStruct(tokens.shape, BF16),
        in_specs=[vmem, vmem, hbm],
        out_specs=vmem,
        scratch_shapes=[
            pltpu.VMEM((k1 + K2, hid_cols, CW), BF16),
            pltpu.VMEM((k1, NZ, PLANE, slots, CW), BF16),
            pltpu.VMEM((K2, NZ, PLANE, slots, CW), BF16),
            pltpu.VMEM((k1, 2, PLANE // 2, slots, CW), BF16),
            pltpu.VMEM((k1, 2, PLANE, slots, CW), BF16),
            pltpu.VMEM((k1, PLANE, slots, CW), BF16),
            pltpu.VMEM((k1, PLANE, slots, CW), BF16),
            pltpu.VMEM((K2, NZ, PLANE, slots, CW), BF16),
            pltpu.VMEM((k1, 2 * TOK, CW), F32),
            pltpu.VMEM((k1, TOK, CW), F32),
            pltpu.VMEM((K2, NZ, 2 * TOK, CW), F32),
            pltpu.VMEM((K2, NZ, TOK, CW), F32),
            pltpu.VMEM((K2, NZ, TOK, CW), BF16),
            pltpu.VMEM((K2, 2, TOK // 2, CW), BF16),
            pltpu.VMEM((K2, 2, TOK, CW), BF16),
            dma((k1 + K2,)), dma((k1, 2)), dma((k1, 2)), dma((k1, 2)), dma((k1, 2)),
            dma((k1,)), dma((k1,)), dma((k1,)), dma((k1,)),
            dma((K2,)), dma((K2,)), dma((K2,)), dma((K2,)), dma((K2, 2)), dma((K2, 2)), dma((K2, 2)), dma((K2, 2)),
        ],
        compiler_params=pltpu.CompilerParams(collective_id=1, has_side_effects=True, vmem_limit_bytes=60 << 20),
    )(hid, gpk, w_down[0])


def solution(mesh):
    placed = (
        P(("rep", "head", "side"), None),
        P(("rep", "head", "side"), None),
        P(("rep", "head", "side"), None),
        P(("rep", "head"), None, "side"),
        P(("rep", "head"), None, "side"),
        P(("rep", "head"), "side", None),
    )
    return jax.shard_map(
        on_device,
        mesh=mesh,
        in_specs=placed,
        out_specs=P(("rep", "head", "side"), None),
        check_vma=False,
    )
```

```python
import functools

import jax
import jax.numpy as jnp
from jax import lax
from jax.experimental import pallas as pl
from jax.experimental.pallas import tpu as pltpu
from jax.sharding import PartitionSpec as P

MESH = pl.DeviceIdType.MESH
F32, BF16 = jnp.float32, jnp.bfloat16
CW = 512
K2 = 5
SLOTS1, SLOTS2 = 3, 2
CAP = 8
TOK = 64
NX, NY, NZ = 4, 4, 4
PLANE = NX * NY
OFFS = sorted(
    [(dx, dy) for dx in range(NX) for dy in range(NY) if (dx, dy) != (0, 0)],
    key=lambda off: min(off[0], NX - off[0]) + min(off[1], NY - off[1]),
)


class Place:
    def __init__(self):
        rep = lax.axis_index("rep")
        self.x, self.c = rep // 2, rep % 2
        self.y, self.z = lax.axis_index("head"), lax.axis_index("side")
        self.j = self.x * NY + self.y
        self.up, self.down = lax.rem(self.z + 1, NZ), lax.rem(self.z + NZ - 1, NZ)
        self.core = self.dev(self.x, 1 - self.c, self.y, self.z)
        self.z_up = self.dev(self.x, self.c, self.y, self.up)
        self.z_down = self.dev(self.x, self.c, self.y, self.down)

    def dev(self, x, c, y, z):
        return (x * 2 + c, y, z)

    def plane(self, off):
        x, y = lax.rem(self.x + off[0], NX), lax.rem(self.y + off[1], NY)
        return x * NY + y, self.dev(x, self.c, y, self.z)

    def column(self):
        own = []
        for dc in range(2):
            for dz in range(NZ):
                if (dc, dz) != (0, 0):
                    own.append(self.dev(self.x, lax.rem(self.c + dc, 2), self.y, lax.rem(self.z + dz, NZ)))
        return own


def enter(partners):
    barrier = pltpu.get_barrier_semaphore()
    for device in partners:
        pl.semaphore_signal(barrier, inc=1, device_id=device, device_id_type=MESH)
    pl.semaphore_wait(barrier, len(partners))


def send(src, dst, send_sem, recv_sem, device):
    pltpu.make_async_remote_copy(
        src_ref=src, dst_ref=dst, send_sem=send_sem, recv_sem=recv_sem, device_id=device, device_id_type=MESH
    ).start()


def done(ref, sem):
    pltpu.make_async_copy(ref, ref, sem).wait()


def kernel(
    k1, tok, routes, gates, wg_hbm, wu_hbm, wd_hbm, out,
    meta, metas, tokc, ztok, pk, gpk, out1, out2, x1, x2, w1, w2, acc, hid,
    s1, s2, l1, l2, e1, e2, u2, v1, v2,
    w1_sem, w2_sem, m_send, m_recv, c_send, c_recv, t_send, t_recv, tc_send, tc_recv,
    a1_send, a1_recv, z_send, z_recv, f_send, f_recv, a2_send, a2_recv,
    s1_send, s1_recv, s2_send, s2_recv, b1_send, b1_recv, e1_send, e1_recv,
    b2_send, b2_recv, e2_send, e2_recv, v1_send, v1_recv, v2_send, v2_recv,
):
    y1, y2, r1, t1, t2 = x1, x2, out1, tokc, ztok
    me = Place()
    d1 = k1 * CW
    half = TOK // 2
    low, high = pl.ds(0, PLANE // 2), pl.ds(PLANE // 2, PLANE // 2)
    across = lax.rem(me.z + 2, NZ)
    own_rows = pl.ds(pl.multiple_of(me.c * TOK, TOK), TOK)
    core_rows = pl.ds(pl.multiple_of((1 - me.c) * TOK, TOK), TOK)

    def load_in(w, sem, slot, kk):
        rows = pl.ds(pl.multiple_of(kk * CW, CW), CW)
        pltpu.make_async_copy(wg_hbm.at[rows], w.at[slot, 0], sem.at[slot, 0]).start()
        pltpu.make_async_copy(wu_hbm.at[rows], w.at[slot, 1], sem.at[slot, 1]).start()

    def load_down(w, sem, slot, kk):
        cols = pl.ds(pl.multiple_of(kk * CW, CW), CW)
        pltpu.make_async_copy(wd_hbm.at[:, cols], w.at[slot, 0], sem.at[slot, 0]).start()

    for k in range(SLOTS1):
        load_in(w1, w1_sem, k, k)
    for m in range(SLOTS2):
        load_in(w2, w2_sem, m, k1 + m)
    experts = 2 * PLANE
    expert = lax.broadcasted_iota(jnp.int32, (experts, TOK), 0)
    named = [jnp.where(expert == routes[i:i + 1, :], 1.0, 0.0) for i in range(2)]
    earlier = lax.broadcasted_iota(jnp.int32, (TOK, TOK), 0) < lax.broadcasted_iota(jnp.int32, (TOK, TOK), 1)
    before = jnp.dot((named[0] + named[1]).astype(BF16), jnp.where(earlier, 1.0, 0.0).astype(BF16), preferred_element_type=F32)
    parts = []
    for i in range(2):
        slot = jnp.sum(before * named[i], axis=0, keepdims=True)
        parts.append(routes[i:i + 1, :].astype(F32) * CAP + slot)
    parts += [gates[0:1, :], gates[1:2, :], jnp.zeros((4, TOK), F32)]
    own = jnp.concatenate(parts, axis=0)
    lane_core = lax.broadcasted_iota(jnp.int32, (8, 2 * TOK), 1) // TOK
    meta[...] = jnp.where(lane_core == me.c, jnp.concatenate([own, own], axis=1), 0.0)
    enter([me.plane(off)[1] for off in OFFS] + me.column())

    own_meta = metas.at[me.z, me.c]
    pltpu.make_async_copy(meta, own_meta, m_recv).start()
    for i, device in enumerate(me.column()):
        send(meta, own_meta, m_send.at[i], m_recv, device)
    tail = pl.ds(d1, K2 * CW)
    own_tok = ztok.at[me.z, own_rows]
    send(tok.at[:, tail], own_tok, t_send.at[0], t_recv.at[0], me.z_up)
    send(tok.at[:, tail], own_tok, t_send.at[1], t_recv.at[1], me.z_down)
    for k in range(k1):
        cols = pl.ds(k * CW, CW)
        send(tok.at[:, cols], tokc.at[k, own_rows], c_send.at[k], c_recv.at[k], me.core)
        pltpu.make_async_copy(tok.at[:, cols], tokc.at[k, own_rows], c_recv.at[k]).start()
    pltpu.make_async_copy(tok.at[:, tail], own_tok, t_recv.at[4]).start()

    def hits(zz):
        shape = (2 * PLANE * CAP, 2 * TOK)
        row = lax.broadcasted_iota(jnp.int32, shape, 0)
        col = lax.broadcasted_iota(jnp.int32, shape, 1)
        dest = row // (2 * CAP)
        want = ((2 * (dest // NY) + me.c) * NY + dest % NY) * CAP + row % CAP
        want = jnp.where((row // CAP) % 2 == col // TOK, want, -1).astype(F32)
        both = metas[zz, 0] + metas[zz, 1]
        return both, want == both[0:1], want == both[1:2]

    def pickers(zz):
        _, hit0, hit1 = hits(zz)
        pk[zz] = jnp.where(hit0 | hit1, 1.0, 0.0).astype(BF16)

    def gated_pickers(zz):
        both, hit0, hit1 = hits(zz)
        gated = jnp.where(hit0, both[2:3], 0.0) + jnp.where(hit1, both[3:4], 0.0)
        gated = gated.T
        high = gated.astype(BF16)
        gpk[zz, 0] = high
        gpk[zz, 1] = (gated - high.astype(F32)).astype(BF16)

    done(metas, m_recv)
    pickers(me.z)

    def p1_issue(k):
        done(tokc.at[k], c_recv.at[k])
        picked = jnp.dot(pk[me.z], tokc[k], preferred_element_type=F32)
        out1[k] = picked.astype(BF16).reshape(PLANE, 2 * CAP, CW)
        here = x1.at[k, me.z, me.j]
        for off in OFFS:
            j, device = me.plane(off)
            send(out1.at[k, j], here, a1_send.at[k], a1_recv.at[k], device)
        pltpu.make_async_copy(out1.at[k, me.j], here, a1_recv.at[k]).start()

    def z_issue(k):
        block = x1.at[k, me.z]
        done(block, a1_recv.at[k])
        send(block, block, z_send.at[k, 0], z_recv.at[k, 0], me.z_up)
        send(block, block, z_send.at[k, 1], z_recv.at[k, 1], me.z_down)

    def z_forward(k):
        done(x1.at[k, me.down], z_recv.at[k, 0])
        part = x1.at[k, me.down, low]
        send(part, part, f_send.at[k, 0], f_recv.at[k, 0], me.z_up)
        done(x1.at[k, me.up], z_recv.at[k, 1])
        part = x1.at[k, me.up, high]
        send(part, part, f_send.at[k, 1], f_recv.at[k, 1], me.z_down)

    def project(block, w, sem, slot):
        hid_cols = hid.shape[1]
        for i in range(2):
            done(w.at[slot, i], sem.at[slot, i])

            @pl.loop(0, hid_cols // 256)
            def _(n):
                cols = pl.ds(pl.multiple_of(n * 256, 256), 256)
                to = pl.ds(pl.multiple_of(i * hid_cols + n * 256, 256), 256)
                part = jnp.dot(block[...].reshape(acc.shape[0], CW), w[slot, i, :, cols], preferred_element_type=F32)
                acc[:, to] = acc[:, to] + part

    def refill(w, sem, n, slots, count, base):
        slot = lax.rem(n, slots)

        @pl.when(n + slots < count)
        def _():
            load_in(w, sem, slot, base + n + slots)

        @pl.when(n + slots >= count)
        def _():
            load_down(w, sem, slot, base + slot)

    def mm1(k):
        done(x1.at[k, across, pl.ds(0, PLANE // 2)], f_recv.at[k, 0])
        done(x1.at[k, across, pl.ds(PLANE // 2, PLANE // 2)], f_recv.at[k, 1])
        project(x1.at[k], w1, w1_sem, lax.rem(k, SLOTS1))
        refill(w1, w1_sem, k, SLOTS1, k1, 0)

    def p2_issue(m):
        cols = pl.ds(pl.multiple_of(m * CW, CW), CW)

        @pl.loop(0, NZ)
        def _(zz):
            picked = jnp.dot(pk[zz], ztok[zz, :, cols], preferred_element_type=F32)
            out2[m, zz] = picked.astype(BF16).reshape(PLANE, 2 * CAP, CW)

        here = x2.at[m, :, me.j]
        for off in OFFS:
            j, device = me.plane(off)
            send(out2.at[m, :, j], here, a2_send.at[m], a2_recv.at[m], device)
        pltpu.make_async_copy(out2.at[m, :, me.j], here, a2_recv.at[m]).start()

    def mm2(m):
        done(x2.at[m], a2_recv.at[m])
        project(x2.at[m], w2, w2_sem, lax.rem(m, SLOTS2))
        refill(w2, w2_sem, m, SLOTS2, K2, k1)

    p1_issue(0)
    p1_issue(1)
    p1_issue(2)
    done(ztok.at[me.down, own_rows], t_recv.at[0])
    part = ztok.at[me.down, pl.ds(pl.multiple_of(me.c * TOK, TOK), half)]
    send(part, part, t_send.at[2], t_recv.at[2], me.z_up)
    done(ztok.at[me.up, own_rows], t_recv.at[1])
    part = ztok.at[me.up, pl.ds(pl.multiple_of(me.c * TOK + half, half), half)]
    send(part, part, t_send.at[3], t_recv.at[3], me.z_down)
    z_issue(0)
    p1_issue(3)
    for dz in range(1, NZ):
        pickers(lax.rem(me.z + dz, NZ))
    z_issue(1)
    done(ztok.at[across, pl.ds(pl.multiple_of(me.c * TOK, TOK), half)], t_recv.at[2])
    done(ztok.at[across, pl.ds(pl.multiple_of(me.c * TOK + half, half), half)], t_recv.at[3])
    done(own_tok, t_recv.at[4])
    mine = ztok.at[:, own_rows]
    send(mine, mine, tc_send, tc_recv, me.core)
    acc[...] = jnp.zeros_like(acc)
    other = ztok.at[:, pl.ds(pl.multiple_of((1 - me.c) * TOK, TOK), TOK)]
    done(other, tc_recv)

    def between(k, lag, count, step):
        @pl.when((k >= lag) & (k < lag + count))
        def _():
            step(k - lag)

    def every_second(k, lag, step):
        @pl.when((k >= lag) & ((k - lag) % 2 == 0) & ((k - lag) // 2 < K2))
        def _():
            step((k - lag) // 2)

    @pl.loop(0, max(k1 + 2, 2 + 2 * K2))
    def _(k):
        @pl.when((k >= 2) & (k < k1))
        def _():
            z_issue(k)

        between(k, 1, k1, z_forward)

        @pl.when(k + 4 < k1)
        def _():
            p1_issue(k + 4)

        every_second(k, 0, p2_issue)
        between(k, 2, NZ, gated_pickers)
        between(k, 2, k1, mm1)
        every_second(k, 3, mm2)

    @pl.loop(0, acc.shape[0] // 128)
    def _(i):
        rows = pl.ds(pl.multiple_of(i * 128, 128), 128)
        hc = hid.shape[1]
        g, u = acc[rows, :hc], acc[rows, hc:]
        hid[rows, :] = (g / (1.0 + jnp.exp(-g)) * u).astype(BF16)

    for i in range(2 * NZ - 1):
        done(meta, m_send.at[i])
    done(tok.at[:, tail], t_send.at[0])
    done(tok.at[:, tail], t_send.at[1])
    done(ztok.at[0, pl.ds(0, half)], t_send.at[2])
    done(ztok.at[0, pl.ds(0, half)], t_send.at[3])
    done(mine, tc_send)

    def left_z(k):
        for side in range(2):
            done(x1.at[k, 0], z_send.at[k, side])
            done(x1.at[k, 0, low], f_send.at[k, side])

    def left_plane(k):
        done(tokc.at[k, pl.ds(0, TOK)], c_send.at[k])
        done(out1.at[k, pl.ds(0, PLANE - 1)], a1_send.at[k])

    def left_tokens(m):
        done(out2.at[m, :, pl.ds(0, PLANE - 1)], a2_send.at[m])

    def down(to, w, sem, n, slots, count, base):
        slot = lax.rem(n, slots)
        done(w.at[slot, 0], sem.at[slot, 0])

        @pl.loop(0, CW // 256)
        def _(i):
            cols = pl.ds(pl.multiple_of(i * 256, 256), 256)
            part = jnp.dot(hid[...], w[slot, 0, :, cols], preferred_element_type=F32)
            to[:, :, :, cols] = part.astype(BF16).reshape(NZ, PLANE, 2 * CAP, 256)

        @pl.when(n + slots < count)
        def _():
            load_down(w, sem, slot, base + n + slots)

    def plus(a, b):
        return (a.astype(F32) + b.astype(F32)).astype(BF16)

    def first(k):
        left_z(k)
        down(y1.at[k], w1, w1_sem, k, SLOTS1, k1, 0)
        send(y1.at[k, across, low], s1.at[k, 0], s1_send.at[k, 0], s1_recv.at[k, 0], me.z_up)
        send(y1.at[k, across, high], s1.at[k, 1], s1_send.at[k, 1], s1_recv.at[k, 1], me.z_down)

    def second(k):
        done(s1.at[k, 0], s1_recv.at[k, 0])
        y1[k, me.up, low] = plus(y1[k, me.up, low], s1[k, 0])
        send(y1.at[k, me.up], s2.at[k, 0], s2_send.at[k, 0], s2_recv.at[k, 0], me.z_up)
        done(s1.at[k, 1], s1_recv.at[k, 1])
        y1[k, me.down, high] = plus(y1[k, me.down, high], s1[k, 1])
        send(y1.at[k, me.down], s2.at[k, 1], s2_send.at[k, 1], s2_recv.at[k, 1], me.z_down)

    def third(k):
        done(s2.at[k, 0], s2_recv.at[k, 0])
        done(s2.at[k, 1], s2_recv.at[k, 1])
        left_plane(k)
        r1[k] = (y1[k, me.z].astype(F32) + s2[k, 0].astype(F32) + s2[k, 1].astype(F32)).astype(BF16)
        here = l1.at[k, me.j]
        for off in OFFS:
            j, device = me.plane(off)
            send(r1.at[k, j], here, b1_send.at[k], b1_recv.at[k], device)
        pltpu.make_async_copy(r1.at[k, me.j], here, b1_recv.at[k]).start()

    def combine(zz, rows):
        rows = rows.reshape(2 * PLANE * CAP, CW)
        return jnp.dot(gpk[zz, 0], rows, preferred_element_type=F32) + jnp.dot(
            gpk[zz, 1], rows, preferred_element_type=F32
        )

    def fourth(k):
        done(l1.at[k], b1_recv.at[k])
        t1[k] = combine(me.z, l1[k]).astype(BF16)
        send(t1.at[k, core_rows], e1.at[k], e1_send.at[k], e1_recv.at[k], me.core)

    def fifth(k):
        done(e1.at[k], e1_recv.at[k])
        out[:, pl.ds(pl.multiple_of(k * CW, CW), CW)] = plus(t1[k, own_rows], e1[k])

    def other_first(m):
        left_tokens(m)
        down(y2.at[m], w2, w2_sem, m, SLOTS2, K2, k1)
        here = l2.at[m, :, me.j]
        for off in OFFS:
            j, device = me.plane(off)
            send(y2.at[m, :, j], here, b2_send.at[m], b2_recv.at[m], device)
        pltpu.make_async_copy(y2.at[m, :, me.j], here, b2_recv.at[m]).start()

    def other_second(m):
        done(l2.at[m], b2_recv.at[m])

        @pl.loop(0, NZ)
        def _(zz):
            t2[zz, :, pl.ds(pl.multiple_of(m * CW, CW), CW)] = combine(zz, l2[m, zz]).astype(BF16)

        send(t2.at[:, core_rows, pl.ds(pl.multiple_of(m * CW, CW), CW)], e2.at[m], e2_send.at[m], e2_recv.at[m], me.core)

    def other_third(m):
        done(e2.at[m], e2_recv.at[m])
        for zz in range(NZ):
            u2[m, zz] = plus(t2[zz, own_rows, pl.ds(pl.multiple_of(m * CW, CW), CW)], e2[m, zz])
        send(u2.at[m, across, pl.ds(0, half)], v1.at[m, 0], v1_send.at[m, 0], v1_recv.at[m, 0], me.z_up)
        send(u2.at[m, across, pl.ds(half, half)], v1.at[m, 1], v1_send.at[m, 1], v1_recv.at[m, 1], me.z_down)

    def other_fourth(m):
        done(v1.at[m, 0], v1_recv.at[m, 0])
        u2[m, me.up, :half] = plus(u2[m, me.up, :half], v1[m, 0])
        send(u2.at[m, me.up], v2.at[m, 0], v2_send.at[m, 0], v2_recv.at[m, 0], me.z_up)
        done(v1.at[m, 1], v1_recv.at[m, 1])
        u2[m, me.down, half:] = plus(u2[m, me.down, half:], v1[m, 1])
        send(u2.at[m, me.down], v2.at[m, 1], v2_send.at[m, 1], v2_recv.at[m, 1], me.z_down)

    def other_fifth(m):
        done(v2.at[m, 0], v2_recv.at[m, 0])
        done(v2.at[m, 1], v2_recv.at[m, 1])
        total = u2[m, me.z].astype(F32) + v2[m, 0].astype(F32) + v2[m, 1].astype(F32)
        out[:, pl.ds(pl.multiple_of((k1 + m) * CW, CW), CW)] = total.astype(BF16)

    @pl.loop(0, max(k1 + 7, 4 + 2 * K2))
    def _(k):
        between(k, 0, k1, first)
        between(k, 2, k1, second)
        between(k, 0, K2, other_first)
        between(k, 3, k1, third)
        every_second(k, 2, other_second)
        every_second(k, 3, other_third)
        every_second(k, 4, other_fourth)
        every_second(k, 5, other_fifth)
        between(k, 6, k1, fourth)
        between(k, 7, k1, fifth)

    @pl.loop(0, k1)
    def _(k):
        for side in range(2):
            done(s1.at[k, 0], s1_send.at[k, side])
            done(s2.at[k, 0], s2_send.at[k, side])
        done(r1.at[k, pl.ds(0, PLANE - 1)], b1_send.at[k])
        done(e1.at[k], e1_send.at[k])

    @pl.loop(0, K2)
    def _(m):
        done(y2.at[m, :, pl.ds(0, PLANE - 1)], b2_send.at[m])
        done(e2.at[m], e2_send.at[m])
        for side in range(2):
            done(v1.at[m, 0], v1_send.at[m, side])
            done(v2.at[m, 0], v2_send.at[m, side])


def on_device(tokens, routes, gates, w_gate, w_up, w_down):
    width = tokens.shape[1]
    k1 = width // CW - K2
    hid_cols = w_gate.shape[2]
    rows = NZ * PLANE * 2 * CAP
    slots = 2 * CAP

    def dma(*shape):
        return pltpu.SemaphoreType.DMA(shape)

    vmem = pl.BlockSpec(memory_space=pltpu.VMEM)
    hbm = pl.BlockSpec(memory_space=pl.ANY)
    return pl.pallas_call(
        functools.partial(kernel, k1),
        out_shape=jax.ShapeDtypeStruct(tokens.shape, BF16),
        in_specs=[vmem, vmem, vmem, hbm, hbm, hbm],
        out_specs=vmem,
        scratch_shapes=[
            pltpu.VMEM((8, 2 * TOK), F32),
            pltpu.VMEM((NZ, 2, 8, 2 * TOK), F32),
            pltpu.VMEM((k1, 2 * TOK, CW), BF16),
            pltpu.VMEM((NZ, 2 * TOK, K2 * CW), BF16),
            pltpu.VMEM((NZ, PLANE * slots, 2 * TOK), BF16),
            pltpu.VMEM((NZ, 2, 2 * TOK, PLANE * slots), BF16),
            pltpu.VMEM((k1, PLANE, slots, CW), BF16),
            pltpu.VMEM((K2, NZ, PLANE, slots, CW), BF16),
            pltpu.VMEM((k1, NZ, PLANE, slots, CW), BF16),
            pltpu.VMEM((K2, NZ, PLANE, slots, CW), BF16),
            pltpu.VMEM((SLOTS1, 2, CW, hid_cols), BF16),
            pltpu.VMEM((SLOTS2, 2, CW, hid_cols), BF16),
            pltpu.VMEM((rows, 2 * hid_cols), F32),
            pltpu.VMEM((rows, hid_cols), BF16),
            pltpu.VMEM((k1, 2, PLANE // 2, slots, CW), BF16),
            pltpu.VMEM((k1, 2, PLANE, slots, CW), BF16),
            pltpu.VMEM((k1, PLANE, slots, CW), BF16),
            pltpu.VMEM((K2, NZ, PLANE, slots, CW), BF16),
            pltpu.VMEM((k1, TOK, CW), BF16),
            pltpu.VMEM((K2, NZ, TOK, CW), BF16),
            pltpu.VMEM((K2, NZ, TOK, CW), BF16),
            pltpu.VMEM((K2, 2, TOK // 2, CW), BF16),
            pltpu.VMEM((K2, 2, TOK, CW), BF16),
            dma(SLOTS1, 2), dma(SLOTS2, 2), dma(2 * NZ - 1), pltpu.SemaphoreType.DMA, dma(k1), dma(k1), dma(4), dma(5),
            pltpu.SemaphoreType.DMA, pltpu.SemaphoreType.DMA,
            dma(k1), dma(k1), dma(k1, 2), dma(k1, 2), dma(k1, 2), dma(k1, 2), dma(K2), dma(K2),
            dma(k1, 2), dma(k1, 2), dma(k1, 2), dma(k1, 2), dma(k1), dma(k1), dma(k1), dma(k1),
            dma(K2), dma(K2), dma(K2), dma(K2), dma(K2, 2), dma(K2, 2), dma(K2, 2), dma(K2, 2),
        ],
        compiler_params=pltpu.CompilerParams(collective_id=0, has_side_effects=True, vmem_limit_bytes=61 << 20),
    )(tokens, routes.T, gates.T, w_gate[0], w_up[0], w_down[0])


def solution(mesh):
    placed = (
        P(("rep", "head", "side"), None),
        P(("rep", "head", "side"), None),
        P(("rep", "head", "side"), None),
        P(("rep", "head"), None, "side"),
        P(("rep", "head"), None, "side"),
        P(("rep", "head"), "side", None),
    )
    return jax.shard_map(
        on_device,
        mesh=mesh,
        in_specs=placed,
        out_specs=P(("rep", "head", "side"), None),
        check_vma=False,
    )
```

```python
import functools

import jax
import jax.numpy as jnp
from jax import lax
from jax.experimental import pallas as pl
from jax.experimental.pallas import tpu as pltpu
from jax.sharding import PartitionSpec as P

MESH = pl.DeviceIdType.MESH
F32, BF16 = jnp.float32, jnp.bfloat16
CW = 512
K2 = 5
SLOTS1, SLOTS2 = 3, 3
CAP = 8
TOK = 64
NX, NY, NZ = 4, 4, 4
PLANE = NX * NY
OFFS = sorted(
    [(dx, dy) for dx in range(NX) for dy in range(NY) if (dx, dy) != (0, 0)],
    key=lambda off: min(off[0], NX - off[0]) + min(off[1], NY - off[1]),
)


class Place:
    def __init__(self):
        rep = lax.axis_index("rep")
        self.x, self.c = rep // 2, rep % 2
        self.y, self.z = lax.axis_index("head"), lax.axis_index("side")
        self.j = self.x * NY + self.y
        self.up, self.down = lax.rem(self.z + 1, NZ), lax.rem(self.z + NZ - 1, NZ)
        self.core = self.dev(self.x, 1 - self.c, self.y, self.z)
        self.z_up = self.dev(self.x, self.c, self.y, self.up)
        self.z_down = self.dev(self.x, self.c, self.y, self.down)

    def dev(self, x, c, y, z):
        return (x * 2 + c, y, z)

    def plane(self, off):
        x, y = lax.rem(self.x + off[0], NX), lax.rem(self.y + off[1], NY)
        return x * NY + y, self.dev(x, self.c, y, self.z)

    def column(self):
        own = []
        for dc in range(2):
            for dz in range(NZ):
                if (dc, dz) != (0, 0):
                    own.append(self.dev(self.x, lax.rem(self.c + dc, 2), self.y, lax.rem(self.z + dz, NZ)))
        return own


def enter(partners):
    barrier = pltpu.get_barrier_semaphore()
    for device in partners:
        pl.semaphore_signal(barrier, inc=1, device_id=device, device_id_type=MESH)
    pl.semaphore_wait(barrier, len(partners))


def send(src, dst, send_sem, recv_sem, device):
    pltpu.make_async_remote_copy(
        src_ref=src, dst_ref=dst, send_sem=send_sem, recv_sem=recv_sem, device_id=device, device_id_type=MESH
    ).start()


def done(ref, sem):
    pltpu.make_async_copy(ref, ref, sem).wait()


def kernel(
    k1, tok, routes, gates, wg_hbm, wu_hbm, wd_hbm, out,
    meta, metas, tokc, ztok, pk, gpk, out1, out2, x1, x2, w1, w2, acc, hid,
    s1, s2, l1, l2, e1, e2, u2, v1, v2,
    w1_sem, w2_sem, m_send, m_recv, c_send, c_recv, t_send, t_recv, tc_send, tc_recv,
    a1_send, a1_recv, z_send, z_recv, f_send, f_recv, a2_send, a2_recv,
    s1_send, s1_recv, s2_send, s2_recv, b1_send, b1_recv, e1_send, e1_recv,
    b2_send, b2_recv, e2_send, e2_recv, v1_send, v1_recv, v2_send, v2_recv,
):
    y1, y2, r1, t1, t2 = x1, x2, out1, tokc, ztok
    me = Place()
    d1 = k1 * CW
    half = TOK // 2
    low, high = pl.ds(0, PLANE // 2), pl.ds(PLANE // 2, PLANE // 2)
    across = lax.rem(me.z + 2, NZ)
    own_rows = pl.ds(pl.multiple_of(me.c * TOK, TOK), TOK)
    core_rows = pl.ds(pl.multiple_of((1 - me.c) * TOK, TOK), TOK)

    def load_in(w, sem, slot, kk):
        rows = pl.ds(pl.multiple_of(kk * CW, CW), CW)
        pltpu.make_async_copy(wg_hbm.at[rows], w.at[slot, 0], sem.at[slot, 0]).start()
        pltpu.make_async_copy(wu_hbm.at[rows], w.at[slot, 1], sem.at[slot, 1]).start()

    def load_down(w, sem, slot, kk):
        cols = pl.ds(pl.multiple_of(kk * CW, CW), CW)
        pltpu.make_async_copy(wd_hbm.at[:, cols], w.at[slot, 0], sem.at[slot, 0]).start()

    for k in range(SLOTS1):
        load_in(w1, w1_sem, k, k)
    for m in range(SLOTS2):
        load_in(w2, w2_sem, m, k1 + m)
    experts = 2 * PLANE
    expert = lax.broadcasted_iota(jnp.int32, (experts, TOK), 0)
    named = [jnp.where(expert == routes[i:i + 1, :], 1.0, 0.0) for i in range(2)]
    earlier = lax.broadcasted_iota(jnp.int32, (TOK, TOK), 0) < lax.broadcasted_iota(jnp.int32, (TOK, TOK), 1)
    before = jnp.dot((named[0] + named[1]).astype(BF16), jnp.where(earlier, 1.0, 0.0).astype(BF16), preferred_element_type=F32)
    parts = []
    for i in range(2):
        slot = jnp.sum(before * named[i], axis=0, keepdims=True)
        parts.append(routes[i:i + 1, :].astype(F32) * CAP + slot)
    parts += [gates[0:1, :], gates[1:2, :], jnp.zeros((4, TOK), F32)]
    own = jnp.concatenate(parts, axis=0)
    lane_core = lax.broadcasted_iota(jnp.int32, (8, 2 * TOK), 1) // TOK
    meta[...] = jnp.where(lane_core == me.c, jnp.concatenate([own, own], axis=1), 0.0)
    enter([me.plane(off)[1] for off in OFFS] + me.column())

    own_meta = metas.at[me.z, me.c]
    pltpu.make_async_copy(meta, own_meta, m_recv).start()
    for i, device in enumerate(me.column()):
        send(meta, own_meta, m_send.at[i], m_recv, device)
    tail = pl.ds(d1, K2 * CW)
    own_tok = ztok.at[me.z, own_rows]
    send(tok.at[:, tail], own_tok, t_send.at[0], t_recv.at[0], me.z_up)
    send(tok.at[:, tail], own_tok, t_send.at[1], t_recv.at[1], me.z_down)
    for k in range(k1):
        cols = pl.ds(k * CW, CW)
        send(tok.at[:, cols], tokc.at[k, own_rows], c_send.at[k], c_recv.at[k], me.core)
        pltpu.make_async_copy(tok.at[:, cols], tokc.at[k, own_rows], c_recv.at[k]).start()
    pltpu.make_async_copy(tok.at[:, tail], own_tok, t_recv.at[4]).start()

    def hits(zz):
        shape = (2 * PLANE * CAP, 2 * TOK)
        row = lax.broadcasted_iota(jnp.int32, shape, 0)
        col = lax.broadcasted_iota(jnp.int32, shape, 1)
        dest = row // (2 * CAP)
        want = ((2 * (dest // NY) + me.c) * NY + dest % NY) * CAP + row % CAP
        want = jnp.where((row // CAP) % 2 == col // TOK, want, -1).astype(F32)
        both = metas[zz, 0] + metas[zz, 1]
        return both, want == both[0:1], want == both[1:2]

    def pickers(zz):
        _, hit0, hit1 = hits(zz)
        pk[zz] = jnp.where(hit0 | hit1, 1.0, 0.0).astype(BF16)

    def gated_pickers(zz):
        both, hit0, hit1 = hits(zz)
        gated = jnp.where(hit0, both[2:3], 0.0) + jnp.where(hit1, both[3:4], 0.0)
        gated = gated.T
        high = gated.astype(BF16)
        gpk[zz, 0] = high
        gpk[zz, 1] = (gated - high.astype(F32)).astype(BF16)

    done(metas, m_recv)
    pickers(me.z)

    def p1_issue(k):
        done(tokc.at[k], c_recv.at[k])
        picked = jnp.dot(pk[me.z], tokc[k], preferred_element_type=F32)
        out1[k] = picked.astype(BF16).reshape(PLANE, 2 * CAP, CW)
        here = x1.at[k, me.z, me.j]
        for off in OFFS:
            j, device = me.plane(off)
            send(out1.at[k, j], here, a1_send.at[k], a1_recv.at[k], device)
        pltpu.make_async_copy(out1.at[k, me.j], here, a1_recv.at[k]).start()

    def z_issue(k):
        block = x1.at[k, me.z]
        done(block, a1_recv.at[k])
        send(block, block, z_send.at[k, 0], z_recv.at[k, 0], me.z_up)
        send(block, block, z_send.at[k, 1], z_recv.at[k, 1], me.z_down)

    def z_forward(k):
        done(x1.at[k, me.down], z_recv.at[k, 0])
        part = x1.at[k, me.down, low]
        send(part, part, f_send.at[k, 0], f_recv.at[k, 0], me.z_up)
        done(x1.at[k, me.up], z_recv.at[k, 1])
        part = x1.at[k, me.up, high]
        send(part, part, f_send.at[k, 1], f_recv.at[k, 1], me.z_down)

    def project(block, w, sem, slot):
        hid_cols = hid.shape[1]
        for i in range(2):
            done(w.at[slot, i], sem.at[slot, i])

            @pl.loop(0, hid_cols // 256)
            def _(n):
                cols = pl.ds(pl.multiple_of(n * 256, 256), 256)
                to = pl.ds(pl.multiple_of(i * hid_cols + n * 256, 256), 256)
                part = jnp.dot(block[...].reshape(acc.shape[0], CW), w[slot, i, :, cols], preferred_element_type=F32)
                acc[:, to] = acc[:, to] + part

    def refill(w, sem, n, slots, count, base):
        slot = lax.rem(n, slots)

        @pl.when(n + slots < count)
        def _():
            load_in(w, sem, slot, base + n + slots)

        @pl.when(n + slots >= count)
        def _():
            load_down(w, sem, slot, base + slot)

    def mm1(k):
        done(x1.at[k, across, pl.ds(0, PLANE // 2)], f_recv.at[k, 0])
        done(x1.at[k, across, pl.ds(PLANE // 2, PLANE // 2)], f_recv.at[k, 1])
        project(x1.at[k], w1, w1_sem, lax.rem(k, SLOTS1))
        refill(w1, w1_sem, k, SLOTS1, k1, 0)

    def p2_issue(m):
        cols = pl.ds(pl.multiple_of(m * CW, CW), CW)

        @pl.loop(0, NZ)
        def _(zz):
            picked = jnp.dot(pk[zz], ztok[zz, :, cols], preferred_element_type=F32)
            out2[m, zz] = picked.astype(BF16).reshape(PLANE, 2 * CAP, CW)

        here = x2.at[m, :, me.j]
        for off in OFFS:
            j, device = me.plane(off)
            send(out2.at[m, :, j], here, a2_send.at[m], a2_recv.at[m], device)
        pltpu.make_async_copy(out2.at[m, :, me.j], here, a2_recv.at[m]).start()

    def mm2(m):
        done(x2.at[m], a2_recv.at[m])
        project(x2.at[m], w2, w2_sem, lax.rem(m, SLOTS2))
        refill(w2, w2_sem, m, SLOTS2, K2, k1)

    p1_issue(0)
    p1_issue(1)
    p1_issue(2)
    done(ztok.at[me.down, own_rows], t_recv.at[0])
    part = ztok.at[me.down, pl.ds(pl.multiple_of(me.c * TOK, TOK), half)]
    send(part, part, t_send.at[2], t_recv.at[2], me.z_up)
    done(ztok.at[me.up, own_rows], t_recv.at[1])
    part = ztok.at[me.up, pl.ds(pl.multiple_of(me.c * TOK + half, half), half)]
    send(part, part, t_send.at[3], t_recv.at[3], me.z_down)
    z_issue(0)
    p1_issue(3)
    for dz in range(1, NZ):
        pickers(lax.rem(me.z + dz, NZ))
    z_issue(1)
    done(ztok.at[across, pl.ds(pl.multiple_of(me.c * TOK, TOK), half)], t_recv.at[2])
    done(ztok.at[across, pl.ds(pl.multiple_of(me.c * TOK + half, half), half)], t_recv.at[3])
    done(own_tok, t_recv.at[4])
    mine = ztok.at[:, own_rows]
    send(mine, mine, tc_send, tc_recv, me.core)
    acc[...] = jnp.zeros_like(acc)
    other = ztok.at[:, pl.ds(pl.multiple_of((1 - me.c) * TOK, TOK), TOK)]
    done(other, tc_recv)

    def between(k, lag, count, step):
        @pl.when((k >= lag) & (k < lag + count))
        def _():
            step(k - lag)

    def every_second(k, lag, step, count):
        @pl.when((k >= lag) & ((k - lag) % 2 == 0) & ((k - lag) // 2 < count))
        def _():
            step((k - lag) // 2)

    @pl.loop(0, max(k1 + 1, 3 + 2 * (K2 - 1)))
    def _(k):
        @pl.when((k >= 2) & (k < k1))
        def _():
            z_issue(k)

        between(k, 1, k1, z_forward)

        @pl.when(k + 4 < k1)
        def _():
            p1_issue(k + 4)

        every_second(k, 0, p2_issue, K2)
        between(k, 2, NZ, gated_pickers)
        between(k, 2, k1 - 1, mm1)
        every_second(k, 4, mm2, K2 - 1)

    for i in range(2 * NZ - 1):
        done(meta, m_send.at[i])
    done(tok.at[:, tail], t_send.at[0])
    done(tok.at[:, tail], t_send.at[1])
    done(ztok.at[0, pl.ds(0, half)], t_send.at[2])
    done(ztok.at[0, pl.ds(0, half)], t_send.at[3])
    done(mine, tc_send)

    def left_z(k):
        for side in range(2):
            done(x1.at[k, 0], z_send.at[k, side])
            done(x1.at[k, 0, low], f_send.at[k, side])

    def left_plane(k):
        done(tokc.at[k, pl.ds(0, TOK)], c_send.at[k])
        done(out1.at[k, pl.ds(0, PLANE - 1)], a1_send.at[k])

    def left_tokens(m):
        done(out2.at[m, :, pl.ds(0, PLANE - 1)], a2_send.at[m])

    def down_block(to, w, slot, zz):
        rows = pl.ds(pl.multiple_of(zz * PLANE * 2 * CAP, PLANE * 2 * CAP), PLANE * 2 * CAP)

        @pl.loop(0, CW // 256)
        def _(i):
            cols = pl.ds(pl.multiple_of(i * 256, 256), 256)
            part = jnp.dot(hid[rows, :], w[slot, 0, :, cols], preferred_element_type=F32)
            to[zz, :, :, cols] = part.astype(BF16).reshape(PLANE, 2 * CAP, 256)

    def down(to, w, sem, n, slots, count, base):
        slot = lax.rem(n, slots)
        done(w.at[slot, 0], sem.at[slot, 0])

        @pl.loop(0, CW // 256)
        def _(i):
            cols = pl.ds(pl.multiple_of(i * 256, 256), 256)
            part = jnp.dot(hid[...], w[slot, 0, :, cols], preferred_element_type=F32)
            to[:, :, :, cols] = part.astype(BF16).reshape(NZ, PLANE, 2 * CAP, 256)

        refill_down(w, sem, n, slots, count, base)

    def refill_down(w, sem, n, slots, count, base):
        @pl.when(n + slots < count)
        def _():
            load_down(w, sem, lax.rem(n, slots), base + n + slots)

    def plus(a, b):
        return (a.astype(F32) + b.astype(F32)).astype(BF16)

    def first_send(k):
        send(y1.at[k, across, low], s1.at[k, 0], s1_send.at[k, 0], s1_recv.at[k, 0], me.z_up)
        send(y1.at[k, across, high], s1.at[k, 1], s1_send.at[k, 1], s1_recv.at[k, 1], me.z_down)

    def first(k):
        left_z(k)
        down(y1.at[k], w1, w1_sem, k, SLOTS1, k1, 0)
        first_send(k)

    def first_across(k):
        left_z(k)
        done(w1.at[k, 0], w1_sem.at[k, 0])
        down_block(y1.at[k], w1, k, across)
        first_send(k)

    def first_rest(k):
        for zz in (me.up, me.down, me.z):
            down_block(y1.at[k], w1, k, zz)
        refill_down(w1, w1_sem, k, SLOTS1, k1, 0)

    def other_block(zz):
        down_block(y2.at[0], w2, 0, zz)
        here = l2.at[0, zz, me.j]
        for off in OFFS:
            j, device = me.plane(off)
            send(y2.at[0, zz, j], here, b2_send.at[0], b2_recv.at[0], device)
        pltpu.make_async_copy(y2.at[0, zz, me.j], here, b2_recv.at[0]).start()

    end1, end2 = (k1 - 1) % SLOTS1, (K2 - 1) % SLOTS2
    block_rows = PLANE * 2 * CAP

    def add_block(zz):
        rows = pl.ds(pl.multiple_of(zz * block_rows, block_rows), block_rows)
        for i in range(2):
            @pl.loop(0, hid.shape[1] // 256)
            def _(n):
                cols = pl.ds(pl.multiple_of(n * 256, 256), 256)
                to = pl.ds(pl.multiple_of(i * hid.shape[1] + n * 256, 256), 256)
                x = x1[k1 - 1, zz].reshape(block_rows, CW)
                acc[rows, to] = acc[rows, to] + jnp.dot(x, w1[end1, i, :, cols], preferred_element_type=F32)

    def finish_block(zz):
        rows = pl.ds(pl.multiple_of(zz * block_rows, block_rows), block_rows)

        @pl.loop(0, hid.shape[1] // 256)
        def _(n):
            cols = pl.ds(pl.multiple_of(n * 256, 256), 256)
            more = pl.ds(pl.multiple_of(hid.shape[1] + n * 256, 256), 256)
            x = x2[K2 - 1, zz].reshape(block_rows, CW)
            g = acc[rows, cols] + jnp.dot(x, w2[end2, 0, :, cols], preferred_element_type=F32)
            u = acc[rows, more] + jnp.dot(x, w2[end2, 1, :, cols], preferred_element_type=F32)
            hid[rows, cols] = (g / (1.0 + jnp.exp(-g)) * u).astype(BF16)

    for i in range(2):
        done(w1.at[end1, i], w1_sem.at[end1, i])
        done(w2.at[end2, i], w2_sem.at[end2, i])
    for zz in (me.z, me.up, me.down):
        add_block(zz)
    done(x1.at[k1 - 1, across, low], f_recv.at[k1 - 1, 0])
    done(x1.at[k1 - 1, across, high], f_recv.at[k1 - 1, 1])
    add_block(across)
    load_down(w1, w1_sem, end1, end1)
    done(x2.at[K2 - 1], a2_recv.at[K2 - 1])
    finish_block(across)
    first_across(0)
    left_tokens(0)
    done(w2.at[0, 0], w2_sem.at[0, 0])
    other_block(across)
    first_across(1)
    for zz in (me.up, me.down, me.z):
        finish_block(zz)
    load_down(w2, w2_sem, end2, k1 + end2)
    first_rest(0)
    for zz in (me.up, me.down, me.z):
        other_block(zz)
    refill_down(w2, w2_sem, 0, SLOTS2, K2, k1)
    first_rest(1)

    def second(k):
        done(s1.at[k, 0], s1_recv.at[k, 0])
        y1[k, me.up, low] = plus(y1[k, me.up, low], s1[k, 0])
        send(y1.at[k, me.up], s2.at[k, 0], s2_send.at[k, 0], s2_recv.at[k, 0], me.z_up)
        done(s1.at[k, 1], s1_recv.at[k, 1])
        y1[k, me.down, high] = plus(y1[k, me.down, high], s1[k, 1])
        send(y1.at[k, me.down], s2.at[k, 1], s2_send.at[k, 1], s2_recv.at[k, 1], me.z_down)

    def third(k):
        done(s2.at[k, 0], s2_recv.at[k, 0])
        done(s2.at[k, 1], s2_recv.at[k, 1])
        left_plane(k)
        r1[k] = (y1[k, me.z].astype(F32) + s2[k, 0].astype(F32) + s2[k, 1].astype(F32)).astype(BF16)
        here = l1.at[k, me.j]
        for off in OFFS:
            j, device = me.plane(off)
            send(r1.at[k, j], here, b1_send.at[k], b1_recv.at[k], device)
        pltpu.make_async_copy(r1.at[k, me.j], here, b1_recv.at[k]).start()

    def combine(zz, rows):
        rows = rows.reshape(2 * PLANE * CAP, CW)
        return jnp.dot(gpk[zz, 0], rows, preferred_element_type=F32) + jnp.dot(
            gpk[zz, 1], rows, preferred_element_type=F32
        )

    def fourth(k):
        done(l1.at[k], b1_recv.at[k])
        t1[k] = combine(me.z, l1[k]).astype(BF16)
        send(t1.at[k, core_rows], e1.at[k], e1_send.at[k], e1_recv.at[k], me.core)

    def fifth(k):
        done(e1.at[k], e1_recv.at[k])
        out[:, pl.ds(pl.multiple_of(k * CW, CW), CW)] = plus(t1[k, own_rows], e1[k])

    def other_first(m):
        left_tokens(m)
        down(y2.at[m], w2, w2_sem, m, SLOTS2, K2, k1)
        here = l2.at[m, :, me.j]
        for off in OFFS:
            j, device = me.plane(off)
            send(y2.at[m, :, j], here, b2_send.at[m], b2_recv.at[m], device)
        pltpu.make_async_copy(y2.at[m, :, me.j], here, b2_recv.at[m]).start()

    def other_second(m):
        done(l2.at[m], b2_recv.at[m])

        @pl.loop(0, NZ)
        def _(zz):
            t2[zz, :, pl.ds(pl.multiple_of(m * CW, CW), CW)] = combine(zz, l2[m, zz]).astype(BF16)

        send(t2.at[:, core_rows, pl.ds(pl.multiple_of(m * CW, CW), CW)], e2.at[m], e2_send.at[m], e2_recv.at[m], me.core)

    def other_third(m):
        done(e2.at[m], e2_recv.at[m])
        for zz in range(NZ):
            u2[m, zz] = plus(t2[zz, own_rows, pl.ds(pl.multiple_of(m * CW, CW), CW)], e2[m, zz])
        send(u2.at[m, across, pl.ds(0, half)], v1.at[m, 0], v1_send.at[m, 0], v1_recv.at[m, 0], me.z_up)
        send(u2.at[m, across, pl.ds(half, half)], v1.at[m, 1], v1_send.at[m, 1], v1_recv.at[m, 1], me.z_down)

    def other_fourth(m):
        done(v1.at[m, 0], v1_recv.at[m, 0])
        u2[m, me.up, :half] = plus(u2[m, me.up, :half], v1[m, 0])
        send(u2.at[m, me.up], v2.at[m, 0], v2_send.at[m, 0], v2_recv.at[m, 0], me.z_up)
        done(v1.at[m, 1], v1_recv.at[m, 1])
        u2[m, me.down, half:] = plus(u2[m, me.down, half:], v1[m, 1])
        send(u2.at[m, me.down], v2.at[m, 1], v2_send.at[m, 1], v2_recv.at[m, 1], me.z_down)

    def other_fifth(m):
        done(v2.at[m, 0], v2_recv.at[m, 0])
        done(v2.at[m, 1], v2_recv.at[m, 1])
        total = u2[m, me.z].astype(F32) + v2[m, 0].astype(F32) + v2[m, 1].astype(F32)
        out[:, pl.ds(pl.multiple_of((k1 + m) * CW, CW), CW)] = total.astype(BF16)

    def in_pairs(k, lag, step):
        for i in range(2):
            @pl.when((k >= lag) & (2 * (k - lag) + i < k1))
            def _():
                step(2 * (k - lag) + i)

    @pl.loop(0, max(k1 + 6, 2 * K2 + 5))
    def _(k):
        between(k, 2, k1 - 2, lambda i: first(i + 2))
        between(k, 2, k1, second)
        between(k, 0, K2 - 1, lambda i: other_first(i + 1))
        between(k, 3, k1, third)
        for odd in range(2):
            @pl.when((k >= 3) & (k % 3 == odd) & (2 * (k // 3 - 1) + odd < K2))
            def _():
                other_second(2 * (k // 3 - 1) + odd)

        for at, step in ((k1 + 1, other_third), (k1 + 2, other_fourth)):
            @pl.when(k == at)
            def _():
                pl.loop(0, K2)(step)

        in_pairs(k, k1, fourth)

        @pl.when(k == k1 + 4)
        def _():
            pl.loop(0, K2)(other_fifth)

        in_pairs(k, k1 + 1, fifth)

    @pl.loop(0, k1)
    def _(k):
        for side in range(2):
            done(s1.at[k, 0], s1_send.at[k, side])
            done(s2.at[k, 0], s2_send.at[k, side])
        done(r1.at[k, pl.ds(0, PLANE - 1)], b1_send.at[k])
        done(e1.at[k], e1_send.at[k])

    @pl.loop(0, K2)
    def _(m):
        done(y2.at[m, :, pl.ds(0, PLANE - 1)], b2_send.at[m])
        done(e2.at[m], e2_send.at[m])
        for side in range(2):
            done(v1.at[m, 0], v1_send.at[m, side])
            done(v2.at[m, 0], v2_send.at[m, side])


def on_device(tokens, routes, gates, w_gate, w_up, w_down):
    width = tokens.shape[1]
    k1 = width // CW - K2
    hid_cols = w_gate.shape[2]
    rows = NZ * PLANE * 2 * CAP
    slots = 2 * CAP

    def dma(*shape):
        return pltpu.SemaphoreType.DMA(shape)

    vmem = pl.BlockSpec(memory_space=pltpu.VMEM)
    hbm = pl.BlockSpec(memory_space=pl.ANY)
    return pl.pallas_call(
        functools.partial(kernel, k1),
        out_shape=jax.ShapeDtypeStruct(tokens.shape, BF16),
        in_specs=[vmem, vmem, vmem, hbm, hbm, hbm],
        out_specs=vmem,
        scratch_shapes=[
            pltpu.VMEM((8, 2 * TOK), F32),
            pltpu.VMEM((NZ, 2, 8, 2 * TOK), F32),
            pltpu.VMEM((k1, 2 * TOK, CW), BF16),
            pltpu.VMEM((NZ, 2 * TOK, K2 * CW), BF16),
            pltpu.VMEM((NZ, PLANE * slots, 2 * TOK), BF16),
            pltpu.VMEM((NZ, 2, 2 * TOK, PLANE * slots), BF16),
            pltpu.VMEM((k1, PLANE, slots, CW), BF16),
            pltpu.VMEM((K2, NZ, PLANE, slots, CW), BF16),
            pltpu.VMEM((k1, NZ, PLANE, slots, CW), BF16),
            pltpu.VMEM((K2, NZ, PLANE, slots, CW), BF16),
            pltpu.VMEM((SLOTS1, 2, CW, hid_cols), BF16),
            pltpu.VMEM((SLOTS2, 2, CW, hid_cols), BF16),
            pltpu.VMEM((rows, 2 * hid_cols), F32),
            pltpu.VMEM((rows, hid_cols), BF16),
            pltpu.VMEM((k1, 2, PLANE // 2, slots, CW), BF16),
            pltpu.VMEM((k1, 2, PLANE, slots, CW), BF16),
            pltpu.VMEM((k1, PLANE, slots, CW), BF16),
            pltpu.VMEM((K2, NZ, PLANE, slots, CW), BF16),
            pltpu.VMEM((k1, TOK, CW), BF16),
            pltpu.VMEM((K2, NZ, TOK, CW), BF16),
            pltpu.VMEM((K2, NZ, TOK, CW), BF16),
            pltpu.VMEM((K2, 2, TOK // 2, CW), BF16),
            pltpu.VMEM((K2, 2, TOK, CW), BF16),
            dma(SLOTS1, 2), dma(SLOTS2, 2), dma(2 * NZ - 1), pltpu.SemaphoreType.DMA, dma(k1), dma(k1), dma(4), dma(5),
            pltpu.SemaphoreType.DMA, pltpu.SemaphoreType.DMA,
            dma(k1), dma(k1), dma(k1, 2), dma(k1, 2), dma(k1, 2), dma(k1, 2), dma(K2), dma(K2),
            dma(k1, 2), dma(k1, 2), dma(k1, 2), dma(k1, 2), dma(k1), dma(k1), dma(k1), dma(k1),
            dma(K2), dma(K2), dma(K2), dma(K2), dma(K2, 2), dma(K2, 2), dma(K2, 2), dma(K2, 2),
        ],
        compiler_params=pltpu.CompilerParams(collective_id=0, has_side_effects=True, vmem_limit_bytes=61 << 20),
    )(tokens, routes.T, gates.T, w_gate[0], w_up[0], w_down[0])


def solution(mesh):
    placed = (
        P(("rep", "head", "side"), None),
        P(("rep", "head", "side"), None),
        P(("rep", "head", "side"), None),
        P(("rep", "head"), None, "side"),
        P(("rep", "head"), None, "side"),
        P(("rep", "head"), "side", None),
    )
    return jax.shard_map(
        on_device,
        mesh=mesh,
        in_specs=placed,
        out_specs=P(("rep", "head", "side"), None),
        check_vma=False,
    )
```

```python
import functools

import jax
import jax.numpy as jnp
from jax import lax
from jax.experimental import pallas as pl
from jax.experimental.pallas import tpu as pltpu
from jax.sharding import PartitionSpec as P

MESH = pl.DeviceIdType.MESH
F32, BF16 = jnp.float32, jnp.bfloat16
CW = 512
K2 = 5
SLOTS1, SLOTS2 = 3, 3
CAP = 8
TOK = 64
NX, NY, NZ = 4, 4, 4
PLANE = NX * NY
OFFS = sorted(
    [(dx, dy) for dx in range(NX) for dy in range(NY) if (dx, dy) != (0, 0)],
    key=lambda off: min(off[0], NX - off[0]) + min(off[1], NY - off[1]),
)


class Place:
    def __init__(self):
        rep = lax.axis_index("rep")
        self.x, self.c = rep // 2, rep % 2
        self.y, self.z = lax.axis_index("head"), lax.axis_index("side")
        self.j = self.x * NY + self.y
        self.up, self.down = lax.rem(self.z + 1, NZ), lax.rem(self.z + NZ - 1, NZ)
        self.core = self.dev(self.x, 1 - self.c, self.y, self.z)
        self.z_up = self.dev(self.x, self.c, self.y, self.up)
        self.z_down = self.dev(self.x, self.c, self.y, self.down)

    def dev(self, x, c, y, z):
        return (x * 2 + c, y, z)

    def plane(self, off):
        x, y = lax.rem(self.x + off[0], NX), lax.rem(self.y + off[1], NY)
        return x * NY + y, self.dev(x, self.c, y, self.z)

    def column(self):
        own = []
        for dc in range(2):
            for dz in range(NZ):
                if (dc, dz) != (0, 0):
                    own.append(self.dev(self.x, lax.rem(self.c + dc, 2), self.y, lax.rem(self.z + dz, NZ)))
        return own


def greet(partners):
    for device in partners:
        pl.semaphore_signal(pltpu.get_barrier_semaphore(), inc=1, device_id=device, device_id_type=MESH)


def send(src, dst, send_sem, recv_sem, device):
    pltpu.make_async_remote_copy(
        src_ref=src, dst_ref=dst, send_sem=send_sem, recv_sem=recv_sem, device_id=device, device_id_type=MESH
    ).start()


def done(ref, sem):
    pltpu.make_async_copy(ref, ref, sem).wait()


def kernel(
    k1, tok, routes, gates, wg_hbm, wu_hbm, wd_hbm, out,
    meta, metas, tokc, ztok, pk, gpk, out1, out2, x1, x2, w1, w2, acc, hid,
    s1, s2, l1, l2, e1, e2, u2, v1, v2,
    w1_sem, w2_sem, m_send, m_recv, c_send, c_recv, t_send, t_recv, tc_send, tc_recv,
    a1_send, a1_recv, z_send, z_recv, f_send, f_recv, a2_send, a2_recv,
    s1_send, s1_recv, s2_send, s2_recv, b1_send, b1_recv, e1_send, e1_recv,
    b2_send, b2_recv, e2_send, e2_recv, v1_send, v1_recv, v2_send, v2_recv,
):
    y1, y2, r1, t1, t2 = x1, x2, out1, tokc, ztok
    me = Place()
    d1 = k1 * CW
    half = TOK // 2
    low, high = pl.ds(0, PLANE // 2), pl.ds(PLANE // 2, PLANE // 2)
    across = lax.rem(me.z + 2, NZ)
    own_rows = pl.ds(pl.multiple_of(me.c * TOK, TOK), TOK)
    core_rows = pl.ds(pl.multiple_of((1 - me.c) * TOK, TOK), TOK)

    def load_in(w, sem, slot, kk):
        rows = pl.ds(pl.multiple_of(kk * CW, CW), CW)
        pltpu.make_async_copy(wg_hbm.at[rows], w.at[slot, 0], sem.at[slot, 0]).start()
        pltpu.make_async_copy(wu_hbm.at[rows], w.at[slot, 1], sem.at[slot, 1]).start()

    def load_down(w, sem, slot, kk):
        cols = pl.ds(pl.multiple_of(kk * CW, CW), CW)
        pltpu.make_async_copy(wd_hbm.at[:, cols], w.at[slot, 0], sem.at[slot, 0]).start()

    partners = [me.plane(off)[1] for off in OFFS] + me.column()
    greet(partners)
    for k in range(SLOTS1):
        load_in(w1, w1_sem, k, k)
    for m in range(SLOTS2):
        load_in(w2, w2_sem, m, k1 + m)
    experts = 2 * PLANE
    expert = lax.broadcasted_iota(jnp.int32, (experts, TOK), 0)
    named = [jnp.where(expert == routes[i:i + 1, :], 1.0, 0.0) for i in range(2)]
    earlier = lax.broadcasted_iota(jnp.int32, (TOK, TOK), 0) < lax.broadcasted_iota(jnp.int32, (TOK, TOK), 1)
    before = jnp.dot((named[0] + named[1]).astype(BF16), jnp.where(earlier, 1.0, 0.0).astype(BF16), preferred_element_type=F32)
    parts = []
    for i in range(2):
        slot = jnp.sum(before * named[i], axis=0, keepdims=True)
        parts.append(routes[i:i + 1, :].astype(F32) * CAP + slot)
    parts += [gates[0:1, :], gates[1:2, :], jnp.zeros((4, TOK), F32)]
    own = jnp.concatenate(parts, axis=0)
    lane_core = lax.broadcasted_iota(jnp.int32, (8, 2 * TOK), 1) // TOK
    meta[...] = jnp.where(lane_core == me.c, jnp.concatenate([own, own], axis=1), 0.0)
    pl.semaphore_wait(pltpu.get_barrier_semaphore(), len(partners))

    own_meta = metas.at[me.z, me.c]
    pltpu.make_async_copy(meta, own_meta, m_recv).start()
    for i, device in enumerate(me.column()):
        send(meta, own_meta, m_send.at[i], m_recv, device)
    tail = pl.ds(d1, K2 * CW)
    own_tok = ztok.at[me.z, own_rows]
    send(tok.at[:, tail], own_tok, t_send.at[0], t_recv.at[0], me.z_up)
    send(tok.at[:, tail], own_tok, t_send.at[1], t_recv.at[1], me.z_down)
    for k in range(k1):
        cols = pl.ds(k * CW, CW)
        send(tok.at[:, cols], tokc.at[k, own_rows], c_send.at[k], c_recv.at[k], me.core)
        pltpu.make_async_copy(tok.at[:, cols], tokc.at[k, own_rows], c_recv.at[k]).start()
    pltpu.make_async_copy(tok.at[:, tail], own_tok, t_recv.at[4]).start()

    def hits(zz):
        shape = (2 * PLANE * CAP, 2 * TOK)
        row = lax.broadcasted_iota(jnp.int32, shape, 0)
        col = lax.broadcasted_iota(jnp.int32, shape, 1)
        dest = row // (2 * CAP)
        want = ((2 * (dest // NY) + me.c) * NY + dest % NY) * CAP + row % CAP
        want = jnp.where((row // CAP) % 2 == col // TOK, want, -1).astype(F32)
        both = metas[zz, 0] + metas[zz, 1]
        return both, want == both[0:1], want == both[1:2]

    def pickers(zz):
        _, hit0, hit1 = hits(zz)
        pk[zz] = jnp.where(hit0 | hit1, 1.0, 0.0).astype(BF16)

    def gated_pickers(zz):
        both, hit0, hit1 = hits(zz)
        gated = jnp.where(hit0, both[2:3], 0.0) + jnp.where(hit1, both[3:4], 0.0)
        gated = gated.T
        high = gated.astype(BF16)
        gpk[zz, 0] = high
        gpk[zz, 1] = (gated - high.astype(F32)).astype(BF16)

    done(metas, m_recv)
    pickers(me.z)

    def p1_issue(k):
        done(tokc.at[k], c_recv.at[k])
        picked = jnp.dot(pk[me.z], tokc[k], preferred_element_type=F32)
        out1[k] = picked.astype(BF16).reshape(PLANE, 2 * CAP, CW)
        here = x1.at[k, me.z, me.j]
        for off in OFFS:
            j, device = me.plane(off)
            send(out1.at[k, j], here, a1_send.at[k], a1_recv.at[k], device)
        pltpu.make_async_copy(out1.at[k, me.j], here, a1_recv.at[k]).start()

    def z_issue(k):
        block = x1.at[k, me.z]
        done(block, a1_recv.at[k])
        send(block, block, z_send.at[k, 0], z_recv.at[k, 0], me.z_up)
        send(block, block, z_send.at[k, 1], z_recv.at[k, 1], me.z_down)

    def z_forward(k):
        done(x1.at[k, me.down], z_recv.at[k, 0])
        part = x1.at[k, me.down, low]
        send(part, part, f_send.at[k, 0], f_recv.at[k, 0], me.z_up)
        done(x1.at[k, me.up], z_recv.at[k, 1])
        part = x1.at[k, me.up, high]
        send(part, part, f_send.at[k, 1], f_recv.at[k, 1], me.z_down)

    def project(block, w, sem, slot):
        hid_cols = hid.shape[1]
        for i in range(2):
            done(w.at[slot, i], sem.at[slot, i])

            @pl.loop(0, hid_cols // 256)
            def _(n):
                cols = pl.ds(pl.multiple_of(n * 256, 256), 256)
                to = pl.ds(pl.multiple_of(i * hid_cols + n * 256, 256), 256)
                part = jnp.dot(block[...].reshape(acc.shape[0], CW), w[slot, i, :, cols], preferred_element_type=F32)
                acc[:, to] = acc[:, to] + part

    def refill(w, sem, n, slots, count, base):
        slot = lax.rem(n, slots)

        @pl.when(n + slots < count)
        def _():
            load_in(w, sem, slot, base + n + slots)

        @pl.when(n + slots >= count)
        def _():
            load_down(w, sem, slot, base + slot)

    def mm1(k):
        done(x1.at[k, across, pl.ds(0, PLANE // 2)], f_recv.at[k, 0])
        done(x1.at[k, across, pl.ds(PLANE // 2, PLANE // 2)], f_recv.at[k, 1])
        project(x1.at[k], w1, w1_sem, lax.rem(k, SLOTS1))
        refill(w1, w1_sem, k, SLOTS1, k1, 0)

    def p2_issue(m):
        cols = pl.ds(pl.multiple_of(m * CW, CW), CW)

        @pl.loop(0, NZ)
        def _(zz):
            picked = jnp.dot(pk[zz], ztok[zz, :, cols], preferred_element_type=F32)
            out2[m, zz] = picked.astype(BF16).reshape(PLANE, 2 * CAP, CW)

        here = x2.at[m, :, me.j]
        for off in OFFS[::-1]:
            j, device = me.plane(off)
            send(out2.at[m, :, j], here, a2_send.at[m], a2_recv.at[m], device)
        pltpu.make_async_copy(out2.at[m, :, me.j], here, a2_recv.at[m]).start()

    def mm2(m):
        done(x2.at[m], a2_recv.at[m])
        project(x2.at[m], w2, w2_sem, lax.rem(m, SLOTS2))
        refill(w2, w2_sem, m, SLOTS2, K2, k1)

    p1_issue(0)
    p1_issue(1)
    done(ztok.at[me.down, own_rows], t_recv.at[0])
    part = ztok.at[me.down, pl.ds(pl.multiple_of(me.c * TOK, TOK), half)]
    send(part, part, t_send.at[2], t_recv.at[2], me.z_up)
    done(ztok.at[me.up, own_rows], t_recv.at[1])
    part = ztok.at[me.up, pl.ds(pl.multiple_of(me.c * TOK + half, half), half)]
    send(part, part, t_send.at[3], t_recv.at[3], me.z_down)
    z_issue(0)
    p1_issue(2)
    p1_issue(3)
    for dz in range(1, NZ):
        pickers(lax.rem(me.z + dz, NZ))
    z_issue(1)
    done(ztok.at[across, pl.ds(pl.multiple_of(me.c * TOK, TOK), half)], t_recv.at[2])
    done(ztok.at[across, pl.ds(pl.multiple_of(me.c * TOK + half, half), half)], t_recv.at[3])
    done(own_tok, t_recv.at[4])
    mine = ztok.at[:, own_rows]
    send(mine, mine, tc_send, tc_recv, me.core)
    acc[...] = jnp.zeros_like(acc)
    other = ztok.at[:, pl.ds(pl.multiple_of((1 - me.c) * TOK, TOK), TOK)]
    done(other, tc_recv)

    def between(k, lag, count, step):
        @pl.when((k >= lag) & (k < lag + count))
        def _():
            step(k - lag)

    def every_second(k, lag, step, count):
        @pl.when((k >= lag) & ((k - lag) % 2 == 0) & ((k - lag) // 2 < count))
        def _():
            step((k - lag) // 2)

    @pl.loop(0, max(k1 + 1, 3 + 2 * (K2 - 1)))
    def _(k):
        @pl.when((k >= 2) & (k < k1))
        def _():
            z_issue(k)

        between(k, 1, k1, z_forward)

        @pl.when(k + 4 < k1)
        def _():
            p1_issue(k + 4)

        every_second(k, 0, p2_issue, K2)
        between(k, 2, NZ, gated_pickers)
        between(k, 2, k1 - 1, mm1)
        every_second(k, 4, mm2, K2 - 1)

    for i in range(2 * NZ - 1):
        done(meta, m_send.at[i])
    done(tok.at[:, tail], t_send.at[0])
    done(tok.at[:, tail], t_send.at[1])
    done(ztok.at[0, pl.ds(0, half)], t_send.at[2])
    done(ztok.at[0, pl.ds(0, half)], t_send.at[3])
    done(mine, tc_send)

    def left_z(k):
        for side in range(2):
            done(x1.at[k, 0], z_send.at[k, side])
            done(x1.at[k, 0, low], f_send.at[k, side])

    def left_plane(k):
        done(tokc.at[k, pl.ds(0, TOK)], c_send.at[k])
        done(out1.at[k, pl.ds(0, PLANE - 1)], a1_send.at[k])

    def left_tokens(m):
        done(out2.at[m, :, pl.ds(0, PLANE - 1)], a2_send.at[m])

    def down_block(to, w, slot, zz):
        rows = pl.ds(pl.multiple_of(zz * PLANE * 2 * CAP, PLANE * 2 * CAP), PLANE * 2 * CAP)

        @pl.loop(0, CW // 256)
        def _(i):
            cols = pl.ds(pl.multiple_of(i * 256, 256), 256)
            part = jnp.dot(hid[rows, :], w[slot, 0, :, cols], preferred_element_type=F32)
            to[zz, :, :, cols] = part.astype(BF16).reshape(PLANE, 2 * CAP, 256)

    def down(to, w, sem, n, slots, count, base):
        slot = lax.rem(n, slots)
        done(w.at[slot, 0], sem.at[slot, 0])

        @pl.loop(0, CW // 256)
        def _(i):
            cols = pl.ds(pl.multiple_of(i * 256, 256), 256)
            part = jnp.dot(hid[...], w[slot, 0, :, cols], preferred_element_type=F32)
            to[:, :, :, cols] = part.astype(BF16).reshape(NZ, PLANE, 2 * CAP, 256)

        refill_down(w, sem, n, slots, count, base)

    def refill_down(w, sem, n, slots, count, base):
        @pl.when(n + slots < count)
        def _():
            load_down(w, sem, lax.rem(n, slots), base + n + slots)

    def plus(a, b):
        return (a.astype(F32) + b.astype(F32)).astype(BF16)

    def first_send(k):
        send(y1.at[k, across, low], s1.at[k, 0], s1_send.at[k, 0], s1_recv.at[k, 0], me.z_up)
        send(y1.at[k, across, high], s1.at[k, 1], s1_send.at[k, 1], s1_recv.at[k, 1], me.z_down)

    def first(k):
        left_z(k)
        down(y1.at[k], w1, w1_sem, k, SLOTS1, k1, 0)
        first_send(k)

    def second(k):
        done(s1.at[k, 0], s1_recv.at[k, 0])
        y1[k, me.up, low] = plus(y1[k, me.up, low], s1[k, 0])
        send(y1.at[k, me.up], s2.at[k, 0], s2_send.at[k, 0], s2_recv.at[k, 0], me.z_up)
        done(s1.at[k, 1], s1_recv.at[k, 1])
        y1[k, me.down, high] = plus(y1[k, me.down, high], s1[k, 1])
        send(y1.at[k, me.down], s2.at[k, 1], s2_send.at[k, 1], s2_recv.at[k, 1], me.z_down)

    def first_across(k):
        left_z(k)
        done(w1.at[k, 0], w1_sem.at[k, 0])
        down_block(y1.at[k], w1, k, across)
        first_send(k)

    def first_rest(k):
        for zz in (me.up, me.down):
            down_block(y1.at[k], w1, k, zz)
        second(k)

    def other_block(zz):
        down_block(y2.at[0], w2, 0, zz)
        here = l2.at[0, zz, me.j]
        for off in OFFS:
            j, device = me.plane(off)
            send(y2.at[0, zz, j], here, b2_send.at[0], b2_recv.at[0], device)
        pltpu.make_async_copy(y2.at[0, zz, me.j], here, b2_recv.at[0]).start()

    end1, end2 = (k1 - 1) % SLOTS1, (K2 - 1) % SLOTS2
    block_rows = PLANE * 2 * CAP

    def add_block(zz):
        rows = pl.ds(pl.multiple_of(zz * block_rows, block_rows), block_rows)
        for i in range(2):
            @pl.loop(0, hid.shape[1] // 256)
            def _(n):
                cols = pl.ds(pl.multiple_of(n * 256, 256), 256)
                to = pl.ds(pl.multiple_of(i * hid.shape[1] + n * 256, 256), 256)
                x = x1[k1 - 1, zz].reshape(block_rows, CW)
                acc[rows, to] = acc[rows, to] + jnp.dot(x, w1[end1, i, :, cols], preferred_element_type=F32)

    def finish_block(zz):
        rows = pl.ds(pl.multiple_of(zz * block_rows, block_rows), block_rows)

        @pl.loop(0, hid.shape[1] // 256)
        def _(n):
            cols = pl.ds(pl.multiple_of(n * 256, 256), 256)
            more = pl.ds(pl.multiple_of(hid.shape[1] + n * 256, 256), 256)
            x = x2[K2 - 1, zz].reshape(block_rows, CW)
            g = acc[rows, cols] + jnp.dot(x, w2[end2, 0, :, cols], preferred_element_type=F32)
            u = acc[rows, more] + jnp.dot(x, w2[end2, 1, :, cols], preferred_element_type=F32)
            hid[rows, cols] = (g / (1.0 + jnp.exp(-g)) * u).astype(BF16)

    for i in range(2):
        done(w1.at[end1, i], w1_sem.at[end1, i])
        done(w2.at[end2, i], w2_sem.at[end2, i])
    for zz in (me.z, me.up, me.down):
        add_block(zz)
    done(x1.at[k1 - 1, across, low], f_recv.at[k1 - 1, 0])
    done(x1.at[k1 - 1, across, high], f_recv.at[k1 - 1, 1])
    add_block(across)
    load_down(w1, w1_sem, end1, end1)
    done(x2.at[K2 - 1], a2_recv.at[K2 - 1])
    finish_block(across)
    first_across(0)
    left_tokens(0)
    done(w2.at[0, 0], w2_sem.at[0, 0])
    other_block(across)
    first_across(1)
    for zz in (me.up, me.down):
        finish_block(zz)
    first_rest(0)
    finish_block(me.z)
    load_down(w2, w2_sem, end2, k1 + end2)
    for zz in (me.up, me.down, me.z):
        other_block(zz)
    refill_down(w2, w2_sem, 0, SLOTS2, K2, k1)
    first_rest(1)
    for k in range(2):
        down_block(y1.at[k], w1, k, me.z)
        refill_down(w1, w1_sem, k, SLOTS1, k1, 0)

    def third(k):
        done(s2.at[k, 0], s2_recv.at[k, 0])
        done(s2.at[k, 1], s2_recv.at[k, 1])
        left_plane(k)
        r1[k] = (y1[k, me.z].astype(F32) + s2[k, 0].astype(F32) + s2[k, 1].astype(F32)).astype(BF16)
        here = l1.at[k, me.j]
        for off in OFFS:
            j, device = me.plane(off)
            send(r1.at[k, j], here, b1_send.at[k], b1_recv.at[k], device)
        pltpu.make_async_copy(r1.at[k, me.j], here, b1_recv.at[k]).start()

    def combine(zz, rows):
        rows = rows.reshape(2 * PLANE * CAP, CW)
        return jnp.dot(gpk[zz, 0], rows, preferred_element_type=F32) + jnp.dot(
            gpk[zz, 1], rows, preferred_element_type=F32
        )

    def fourth(k):
        done(l1.at[k], b1_recv.at[k])
        t1[k] = combine(me.z, l1[k]).astype(BF16)
        send(t1.at[k, core_rows], e1.at[k], e1_send.at[k], e1_recv.at[k], me.core)

    def fifth(k):
        done(e1.at[k], e1_recv.at[k])
        out[:, pl.ds(pl.multiple_of(k * CW, CW), CW)] = plus(t1[k, own_rows], e1[k])

    def other_first(m):
        left_tokens(m)
        down(y2.at[m], w2, w2_sem, m, SLOTS2, K2, k1)
        here = l2.at[m, :, me.j]
        for off in OFFS:
            j, device = me.plane(off)
            send(y2.at[m, :, j], here, b2_send.at[m], b2_recv.at[m], device)
        pltpu.make_async_copy(y2.at[m, :, me.j], here, b2_recv.at[m]).start()

    def other_second(m):
        done(l2.at[m], b2_recv.at[m])

        @pl.loop(0, NZ)
        def _(zz):
            t2[zz, :, pl.ds(pl.multiple_of(m * CW, CW), CW)] = combine(zz, l2[m, zz]).astype(BF16)

        send(t2.at[:, core_rows, pl.ds(pl.multiple_of(m * CW, CW), CW)], e2.at[m], e2_send.at[m], e2_recv.at[m], me.core)

    def other_third(m):
        done(e2.at[m], e2_recv.at[m])
        for zz in range(NZ):
            u2[m, zz] = plus(t2[zz, own_rows, pl.ds(pl.multiple_of(m * CW, CW), CW)], e2[m, zz])
        send(u2.at[m, across, pl.ds(0, half)], v1.at[m, 0], v1_send.at[m, 0], v1_recv.at[m, 0], me.z_up)
        send(u2.at[m, across, pl.ds(half, half)], v1.at[m, 1], v1_send.at[m, 1], v1_recv.at[m, 1], me.z_down)

    def other_fourth(m):
        done(v1.at[m, 0], v1_recv.at[m, 0])
        u2[m, me.up, :half] = plus(u2[m, me.up, :half], v1[m, 0])
        send(u2.at[m, me.up], v2.at[m, 0], v2_send.at[m, 0], v2_recv.at[m, 0], me.z_up)
        done(v1.at[m, 1], v1_recv.at[m, 1])
        u2[m, me.down, half:] = plus(u2[m, me.down, half:], v1[m, 1])
        send(u2.at[m, me.down], v2.at[m, 1], v2_send.at[m, 1], v2_recv.at[m, 1], me.z_down)

    def other_fifth(m):
        done(v2.at[m, 0], v2_recv.at[m, 0])
        done(v2.at[m, 1], v2_recv.at[m, 1])
        total = u2[m, me.z].astype(F32) + v2[m, 0].astype(F32) + v2[m, 1].astype(F32)
        out[:, pl.ds(pl.multiple_of((k1 + m) * CW, CW), CW)] = total.astype(BF16)

    def in_pairs(k, lag, step):
        for i in range(2):
            @pl.when((k >= lag) & (2 * (k - lag) + i < k1))
            def _():
                step(2 * (k - lag) + i)

    @pl.loop(0, max(k1 + 5, 2 * K2 + 4))
    def _(k):
        between(k, 0, k1 - 2, lambda i: first(i + 2))
        between(k, 2, k1 - 2, lambda i: second(i + 2))
        between(k, 0, K2 - 1, lambda i: other_first(i + 1))
        between(k, 1, k1, third)
        n = k + 1
        for odd in range(2):
            @pl.when((n >= 3) & (n % 3 == odd) & (2 * (n // 3 - 1) + odd < K2))
            def _():
                other_second(2 * (n // 3 - 1) + odd)

        for at, step in ((k1 - 1, other_third), (k1, other_fourth)):
            @pl.when(k == at)
            def _():
                pl.loop(0, K2)(step)

        in_pairs(k, k1 - 1, fourth)

        @pl.when(k == k1 + 3)
        def _():
            pl.loop(0, K2)(other_fifth)

        in_pairs(k, k1, fifth)

    @pl.loop(0, k1)
    def _(k):
        for side in range(2):
            done(s1.at[k, 0], s1_send.at[k, side])
            done(s2.at[k, 0], s2_send.at[k, side])
        done(r1.at[k, pl.ds(0, PLANE - 1)], b1_send.at[k])
        done(e1.at[k], e1_send.at[k])

    @pl.loop(0, K2)
    def _(m):
        done(y2.at[m, :, pl.ds(0, PLANE - 1)], b2_send.at[m])
        done(e2.at[m], e2_send.at[m])
        for side in range(2):
            done(v1.at[m, 0], v1_send.at[m, side])
            done(v2.at[m, 0], v2_send.at[m, side])


def on_device(tokens, routes, gates, w_gate, w_up, w_down):
    width = tokens.shape[1]
    k1 = width // CW - K2
    hid_cols = w_gate.shape[2]
    rows = NZ * PLANE * 2 * CAP
    slots = 2 * CAP

    def dma(*shape):
        return pltpu.SemaphoreType.DMA(shape)

    vmem = pl.BlockSpec(memory_space=pltpu.VMEM)
    hbm = pl.BlockSpec(memory_space=pl.ANY)
    return pl.pallas_call(
        functools.partial(kernel, k1),
        out_shape=jax.ShapeDtypeStruct(tokens.shape, BF16),
        in_specs=[vmem, vmem, vmem, hbm, hbm, hbm],
        out_specs=vmem,
        scratch_shapes=[
            pltpu.VMEM((8, 2 * TOK), F32),
            pltpu.VMEM((NZ, 2, 8, 2 * TOK), F32),
            pltpu.VMEM((k1, 2 * TOK, CW), BF16),
            pltpu.VMEM((NZ, 2 * TOK, K2 * CW), BF16),
            pltpu.VMEM((NZ, PLANE * slots, 2 * TOK), BF16),
            pltpu.VMEM((NZ, 2, 2 * TOK, PLANE * slots), BF16),
            pltpu.VMEM((k1, PLANE, slots, CW), BF16),
            pltpu.VMEM((K2, NZ, PLANE, slots, CW), BF16),
            pltpu.VMEM((k1, NZ, PLANE, slots, CW), BF16),
            pltpu.VMEM((K2, NZ, PLANE, slots, CW), BF16),
            pltpu.VMEM((SLOTS1, 2, CW, hid_cols), BF16),
            pltpu.VMEM((SLOTS2, 2, CW, hid_cols), BF16),
            pltpu.VMEM((rows, 2 * hid_cols), F32),
            pltpu.VMEM((rows, hid_cols), BF16),
            pltpu.VMEM((k1, 2, PLANE // 2, slots, CW), BF16),
            pltpu.VMEM((k1, 2, PLANE, slots, CW), BF16),
            pltpu.VMEM((k1, PLANE, slots, CW), BF16),
            pltpu.VMEM((K2, NZ, PLANE, slots, CW), BF16),
            pltpu.VMEM((k1, TOK, CW), BF16),
            pltpu.VMEM((K2, NZ, TOK, CW), BF16),
            pltpu.VMEM((K2, NZ, TOK, CW), BF16),
            pltpu.VMEM((K2, 2, TOK // 2, CW), BF16),
            pltpu.VMEM((K2, 2, TOK, CW), BF16),
            dma(SLOTS1, 2), dma(SLOTS2, 2), dma(2 * NZ - 1), pltpu.SemaphoreType.DMA, dma(k1), dma(k1), dma(4), dma(5),
            pltpu.SemaphoreType.DMA, pltpu.SemaphoreType.DMA,
            dma(k1), dma(k1), dma(k1, 2), dma(k1, 2), dma(k1, 2), dma(k1, 2), dma(K2), dma(K2),
            dma(k1, 2), dma(k1, 2), dma(k1, 2), dma(k1, 2), dma(k1), dma(k1), dma(k1), dma(k1),
            dma(K2), dma(K2), dma(K2), dma(K2), dma(K2, 2), dma(K2, 2), dma(K2, 2), dma(K2, 2),
        ],
        compiler_params=pltpu.CompilerParams(collective_id=0, has_side_effects=True, vmem_limit_bytes=61 << 20),
    )(tokens, routes.T, gates.T, w_gate[0], w_up[0], w_down[0])


def solution(mesh):
    placed = (
        P(("rep", "head", "side"), None),
        P(("rep", "head", "side"), None),
        P(("rep", "head", "side"), None),
        P(("rep", "head"), None, "side"),
        P(("rep", "head"), None, "side"),
        P(("rep", "head"), "side", None),
    )
    return jax.shard_map(
        on_device,
        mesh=mesh,
        in_specs=placed,
        out_specs=P(("rep", "head", "side"), None),
        check_vma=False,
    )
```

```python
import functools

import jax
import jax.numpy as jnp
from jax import lax
from jax.experimental import pallas as pl
from jax.experimental.pallas import tpu as pltpu
from jax.sharding import PartitionSpec as P

MESH = pl.DeviceIdType.MESH
F32, BF16 = jnp.float32, jnp.bfloat16
CW = 512
K2 = 5
SLOTS1, SLOTS2 = 3, 3
CAP = 8
TOK = 64
NX, NY, NZ = 4, 4, 4
PLANE = NX * NY
OFFS = sorted(
    [(dx, dy) for dx in range(NX) for dy in range(NY) if (dx, dy) != (0, 0)],
    key=lambda off: min(off[0], NX - off[0]) + min(off[1], NY - off[1]),
)


class Place:
    def __init__(self):
        rep = lax.axis_index("rep")
        self.x, self.c = rep // 2, rep % 2
        self.y, self.z = lax.axis_index("head"), lax.axis_index("side")
        self.j = self.x * NY + self.y
        self.up, self.down = lax.rem(self.z + 1, NZ), lax.rem(self.z + NZ - 1, NZ)
        self.core = self.dev(self.x, 1 - self.c, self.y, self.z)
        self.z_up = self.dev(self.x, self.c, self.y, self.up)
        self.z_down = self.dev(self.x, self.c, self.y, self.down)

    def dev(self, x, c, y, z):
        return (x * 2 + c, y, z)

    def plane(self, off):
        x, y = lax.rem(self.x + off[0], NX), lax.rem(self.y + off[1], NY)
        return x * NY + y, self.dev(x, self.c, y, self.z)

    def column(self):
        own = []
        for dc in range(2):
            for dz in range(NZ):
                if (dc, dz) != (0, 0):
                    own.append(self.dev(self.x, lax.rem(self.c + dc, 2), self.y, lax.rem(self.z + dz, NZ)))
        return own


def greet(partners):
    for device in partners:
        pl.semaphore_signal(pltpu.get_barrier_semaphore(), inc=1, device_id=device, device_id_type=MESH)


def send(src, dst, send_sem, recv_sem, device):
    pltpu.make_async_remote_copy(
        src_ref=src, dst_ref=dst, send_sem=send_sem, recv_sem=recv_sem, device_id=device, device_id_type=MESH
    ).start()


def done(ref, sem):
    pltpu.make_async_copy(ref, ref, sem).wait()


def kernel(
    k1, tok, routes, gates, wg_hbm, wu_hbm, wd_hbm, out,
    meta, metas, tokc, ztok, pk, gpk, out1, out2, x1, x2, w1, w2, acc, hid,
    s1, s2, l1, l2, e1, e2, u2, v1, v2,
    w1_sem, w2_sem, m_send, m_recv, c_send, c_recv, t_send, t_recv, tc_send, tc_recv,
    a1_send, a1_recv, z_send, z_recv, f_send, f_recv, a2_send, a2_recv,
    s1_send, s1_recv, s2_send, s2_recv, b1_send, b1_recv, e1_send, e1_recv,
    b2_send, b2_recv, e2_send, e2_recv, v1_send, v1_recv, v2_send, v2_recv,
):
    y1, y2, r1, t1, t2 = x1, x2, out1, tokc, ztok
    me = Place()
    d1 = k1 * CW
    half = TOK // 2
    low, high = pl.ds(0, PLANE // 2), pl.ds(PLANE // 2, PLANE // 2)
    across = lax.rem(me.z + 2, NZ)
    own_rows = pl.ds(pl.multiple_of(me.c * TOK, TOK), TOK)
    core_rows = pl.ds(pl.multiple_of((1 - me.c) * TOK, TOK), TOK)

    def load_in(w, sem, slot, kk):
        rows = pl.ds(pl.multiple_of(kk * CW, CW), CW)
        pltpu.make_async_copy(wg_hbm.at[rows], w.at[slot, 0], sem.at[slot, 0]).start()
        pltpu.make_async_copy(wu_hbm.at[rows], w.at[slot, 1], sem.at[slot, 1]).start()

    def load_down(w, sem, slot, kk):
        cols = pl.ds(pl.multiple_of(kk * CW, CW), CW)
        pltpu.make_async_copy(wd_hbm.at[:, cols], w.at[slot, 0], sem.at[slot, 0]).start()

    partners = [me.plane(off)[1] for off in OFFS] + me.column()
    greet(partners)
    for k in range(SLOTS1):
        load_in(w1, w1_sem, k, k)
    for m in range(SLOTS2):
        load_in(w2, w2_sem, m, k1 + m)
    experts = 2 * PLANE
    expert = lax.broadcasted_iota(jnp.int32, (experts, TOK), 0)
    named = [jnp.where(expert == routes[i:i + 1, :], 1.0, 0.0) for i in range(2)]
    earlier = lax.broadcasted_iota(jnp.int32, (TOK, TOK), 0) < lax.broadcasted_iota(jnp.int32, (TOK, TOK), 1)
    before = jnp.dot((named[0] + named[1]).astype(BF16), jnp.where(earlier, 1.0, 0.0).astype(BF16), preferred_element_type=F32)
    parts = []
    for i in range(2):
        slot = jnp.sum(before * named[i], axis=0, keepdims=True)
        parts.append(routes[i:i + 1, :].astype(F32) * CAP + slot)
    parts += [gates[0:1, :], gates[1:2, :], jnp.zeros((4, TOK), F32)]
    own = jnp.concatenate(parts, axis=0)
    lane_core = lax.broadcasted_iota(jnp.int32, (8, 2 * TOK), 1) // TOK
    meta[...] = jnp.where(lane_core == me.c, jnp.concatenate([own, own], axis=1), 0.0)
    pl.semaphore_wait(pltpu.get_barrier_semaphore(), len(partners))

    own_meta = metas.at[me.z, me.c]
    pltpu.make_async_copy(meta, own_meta, m_recv).start()
    for i, device in enumerate(me.column()):
        send(meta, own_meta, m_send.at[i], m_recv, device)
    tail = pl.ds(d1, K2 * CW)
    own_tok = ztok.at[me.z, own_rows]
    send(tok.at[:, tail], own_tok, t_send.at[0], t_recv.at[0], me.z_up)
    send(tok.at[:, tail], own_tok, t_send.at[1], t_recv.at[1], me.z_down)
    for k in range(k1):
        cols = pl.ds(k * CW, CW)
        send(tok.at[:, cols], tokc.at[k, own_rows], c_send.at[k], c_recv.at[k], me.core)
        pltpu.make_async_copy(tok.at[:, cols], tokc.at[k, own_rows], c_recv.at[k]).start()
    pltpu.make_async_copy(tok.at[:, tail], own_tok, t_recv.at[4]).start()

    def hits(zz):
        shape = (2 * PLANE * CAP, 2 * TOK)
        row = lax.broadcasted_iota(jnp.int32, shape, 0)
        col = lax.broadcasted_iota(jnp.int32, shape, 1)
        dest = row // (2 * CAP)
        want = ((2 * (dest // NY) + me.c) * NY + dest % NY) * CAP + row % CAP
        want = jnp.where((row // CAP) % 2 == col // TOK, want, -1).astype(F32)
        both = metas[zz, 0] + metas[zz, 1]
        return both, want == both[0:1], want == both[1:2]

    def pickers(zz):
        _, hit0, hit1 = hits(zz)
        pk[zz] = jnp.where(hit0 | hit1, 1.0, 0.0).astype(BF16)

    def gated_pickers(zz):
        both, hit0, hit1 = hits(zz)
        gated = jnp.where(hit0, both[2:3], 0.0) + jnp.where(hit1, both[3:4], 0.0)
        gated = gated.T
        high = gated.astype(BF16)
        gpk[zz, 0] = high
        gpk[zz, 1] = (gated - high.astype(F32)).astype(BF16)

    done(metas, m_recv)
    pickers(me.z)

    def p1_issue(k):
        done(tokc.at[k], c_recv.at[k])
        picked = jnp.dot(pk[me.z], tokc[k], preferred_element_type=F32)
        out1[k] = picked.astype(BF16).reshape(PLANE, 2 * CAP, CW)
        here = x1.at[k, me.z, me.j]
        for off in OFFS:
            j, device = me.plane(off)
            send(out1.at[k, j], here, a1_send.at[k], a1_recv.at[k], device)
        pltpu.make_async_copy(out1.at[k, me.j], here, a1_recv.at[k]).start()

    def z_issue(k):
        block = x1.at[k, me.z]
        done(block, a1_recv.at[k])
        send(block, block, z_send.at[k, 0], z_recv.at[k, 0], me.z_up)
        send(block, block, z_send.at[k, 1], z_recv.at[k, 1], me.z_down)

    def z_forward(k):
        done(x1.at[k, me.down], z_recv.at[k, 0])
        part = x1.at[k, me.down, low]
        send(part, part, f_send.at[k, 0], f_recv.at[k, 0], me.z_up)
        done(x1.at[k, me.up], z_recv.at[k, 1])
        part = x1.at[k, me.up, high]
        send(part, part, f_send.at[k, 1], f_recv.at[k, 1], me.z_down)

    def project(block, w, sem, slot):
        hid_cols = hid.shape[1]
        for i in range(2):
            done(w.at[slot, i], sem.at[slot, i])

            @pl.loop(0, hid_cols // 256)
            def _(n):
                cols = pl.ds(pl.multiple_of(n * 256, 256), 256)
                to = pl.ds(pl.multiple_of(i * hid_cols + n * 256, 256), 256)
                part = jnp.dot(block[...].reshape(acc.shape[0], CW), w[slot, i, :, cols], preferred_element_type=F32)
                acc[:, to] = acc[:, to] + part

    def refill(w, sem, n, slots, count, base):
        slot = lax.rem(n, slots)

        @pl.when(n + slots < count)
        def _():
            load_in(w, sem, slot, base + n + slots)

        @pl.when(n + slots >= count)
        def _():
            load_down(w, sem, slot, base + slot)

    def mm1(k):
        done(x1.at[k, across, pl.ds(0, PLANE // 2)], f_recv.at[k, 0])
        done(x1.at[k, across, pl.ds(PLANE // 2, PLANE // 2)], f_recv.at[k, 1])
        project(x1.at[k], w1, w1_sem, lax.rem(k, SLOTS1))
        refill(w1, w1_sem, k, SLOTS1, k1, 0)

    def p2_issue(m):
        cols = pl.ds(pl.multiple_of(m * CW, CW), CW)

        @pl.loop(0, NZ)
        def _(zz):
            picked = jnp.dot(pk[zz], ztok[zz, :, cols], preferred_element_type=F32)
            out2[m, zz] = picked.astype(BF16).reshape(PLANE, 2 * CAP, CW)

        here = x2.at[m, :, me.j]
        for off in OFFS[::-1]:
            j, device = me.plane(off)
            send(out2.at[m, :, j], here, a2_send.at[m], a2_recv.at[m], device)
        pltpu.make_async_copy(out2.at[m, :, me.j], here, a2_recv.at[m]).start()

    def mm2(m):
        done(x2.at[m], a2_recv.at[m])
        project(x2.at[m], w2, w2_sem, lax.rem(m, SLOTS2))
        refill(w2, w2_sem, m, SLOTS2, K2, k1)

    p1_issue(0)
    p1_issue(1)
    done(ztok.at[me.down, own_rows], t_recv.at[0])
    part = ztok.at[me.down, pl.ds(pl.multiple_of(me.c * TOK, TOK), half)]
    send(part, part, t_send.at[2], t_recv.at[2], me.z_up)
    done(ztok.at[me.up, own_rows], t_recv.at[1])
    part = ztok.at[me.up, pl.ds(pl.multiple_of(me.c * TOK + half, half), half)]
    send(part, part, t_send.at[3], t_recv.at[3], me.z_down)
    z_issue(0)
    p1_issue(2)
    p1_issue(3)
    for dz in range(1, NZ):
        pickers(lax.rem(me.z + dz, NZ))
    z_issue(1)
    done(ztok.at[across, pl.ds(pl.multiple_of(me.c * TOK, TOK), half)], t_recv.at[2])
    done(ztok.at[across, pl.ds(pl.multiple_of(me.c * TOK + half, half), half)], t_recv.at[3])
    done(own_tok, t_recv.at[4])
    mine = ztok.at[:, own_rows]
    send(mine, mine, tc_send, tc_recv, me.core)
    acc[...] = jnp.zeros_like(acc)
    other = ztok.at[:, pl.ds(pl.multiple_of((1 - me.c) * TOK, TOK), TOK)]
    done(other, tc_recv)

    def between(k, lag, count, step):
        @pl.when((k >= lag) & (k < lag + count))
        def _():
            step(k - lag)

    def every_second(k, lag, step, count):
        @pl.when((k >= lag) & ((k - lag) % 2 == 0) & ((k - lag) // 2 < count))
        def _():
            step((k - lag) // 2)

    @pl.loop(0, max(k1 + 1, 3 + 2 * (K2 - 1)))
    def _(k):
        @pl.when((k >= 2) & (k < k1))
        def _():
            z_issue(k)

        between(k, 1, k1, z_forward)

        @pl.when(k + 4 < k1)
        def _():
            p1_issue(k + 4)

        every_second(k, 0, p2_issue, K2)
        between(k, 2, NZ, gated_pickers)
        between(k, 2, k1 - 1, mm1)
        every_second(k, 4, mm2, K2 - 1)

    for i in range(2 * NZ - 1):
        done(meta, m_send.at[i])
    done(tok.at[:, tail], t_send.at[0])
    done(tok.at[:, tail], t_send.at[1])
    done(ztok.at[0, pl.ds(0, half)], t_send.at[2])
    done(ztok.at[0, pl.ds(0, half)], t_send.at[3])
    done(mine, tc_send)

    def left_z(k):
        for side in range(2):
            done(x1.at[k, 0], z_send.at[k, side])
            done(x1.at[k, 0, low], f_send.at[k, side])

    def left_plane(k):
        done(tokc.at[k, pl.ds(0, TOK)], c_send.at[k])
        done(out1.at[k, pl.ds(0, PLANE - 1)], a1_send.at[k])

    def left_tokens(m):
        done(out2.at[m, :, pl.ds(0, PLANE - 1)], a2_send.at[m])

    def down_block(to, w, slot, zz):
        rows = pl.ds(pl.multiple_of(zz * PLANE * 2 * CAP, PLANE * 2 * CAP), PLANE * 2 * CAP)

        @pl.loop(0, CW // 256)
        def _(i):
            cols = pl.ds(pl.multiple_of(i * 256, 256), 256)
            part = jnp.dot(hid[rows, :], w[slot, 0, :, cols], preferred_element_type=F32)
            to[zz, :, :, cols] = part.astype(BF16).reshape(PLANE, 2 * CAP, 256)

    def down(to, w, sem, n, slots, count, base):
        slot = lax.rem(n, slots)
        done(w.at[slot, 0], sem.at[slot, 0])

        @pl.loop(0, CW // 256)
        def _(i):
            cols = pl.ds(pl.multiple_of(i * 256, 256), 256)
            part = jnp.dot(hid[...], w[slot, 0, :, cols], preferred_element_type=F32)
            to[:, :, :, cols] = part.astype(BF16).reshape(NZ, PLANE, 2 * CAP, 256)

        refill_down(w, sem, n, slots, count, base)

    def refill_down(w, sem, n, slots, count, base):
        @pl.when(n + slots < count)
        def _():
            load_down(w, sem, lax.rem(n, slots), base + n + slots)

    def plus(a, b):
        return (a.astype(F32) + b.astype(F32)).astype(BF16)

    def first_send(k):
        send(y1.at[k, across, low], s1.at[k, 0], s1_send.at[k, 0], s1_recv.at[k, 0], me.z_up)
        send(y1.at[k, across, high], s1.at[k, 1], s1_send.at[k, 1], s1_recv.at[k, 1], me.z_down)

    def first(k):
        left_z(k)
        down(y1.at[k], w1, w1_sem, k, SLOTS1, k1, 0)
        first_send(k)

    def second(k):
        done(s1.at[k, 0], s1_recv.at[k, 0])
        y1[k, me.up, low] = plus(y1[k, me.up, low], s1[k, 0])
        send(y1.at[k, me.up], s2.at[k, 0], s2_send.at[k, 0], s2_recv.at[k, 0], me.z_up)
        done(s1.at[k, 1], s1_recv.at[k, 1])
        y1[k, me.down, high] = plus(y1[k, me.down, high], s1[k, 1])
        send(y1.at[k, me.down], s2.at[k, 1], s2_send.at[k, 1], s2_recv.at[k, 1], me.z_down)

    def first_across(k):
        left_z(k)
        done(w1.at[k, 0], w1_sem.at[k, 0])
        down_block(y1.at[k], w1, k, across)
        first_send(k)

    def first_rest(k):
        for zz in (me.up, me.down):
            down_block(y1.at[k], w1, k, zz)
        second(k)

    def other_block(zz):
        down_block(y2.at[0], w2, 0, zz)
        here = l2.at[0, zz, me.j]
        for off in OFFS:
            j, device = me.plane(off)
            send(y2.at[0, zz, j], here, b2_send.at[0], b2_recv.at[0], device)
        pltpu.make_async_copy(y2.at[0, zz, me.j], here, b2_recv.at[0]).start()

    end1, end2 = (k1 - 1) % SLOTS1, (K2 - 1) % SLOTS2
    block_rows = PLANE * 2 * CAP

    def add_block(zz):
        rows = pl.ds(pl.multiple_of(zz * block_rows, block_rows), block_rows)
        for i in range(2):
            @pl.loop(0, hid.shape[1] // 256)
            def _(n):
                cols = pl.ds(pl.multiple_of(n * 256, 256), 256)
                to = pl.ds(pl.multiple_of(i * hid.shape[1] + n * 256, 256), 256)
                x = x1[k1 - 1, zz].reshape(block_rows, CW)
                acc[rows, to] = acc[rows, to] + jnp.dot(x, w1[end1, i, :, cols], preferred_element_type=F32)

    def finish_block(zz, both=False):
        rows = pl.ds(pl.multiple_of(zz * block_rows, block_rows), block_rows)

        @pl.loop(0, hid.shape[1] // 256)
        def _(n):
            cols = pl.ds(pl.multiple_of(n * 256, 256), 256)
            more = pl.ds(pl.multiple_of(hid.shape[1] + n * 256, 256), 256)
            x = x2[K2 - 1, zz].reshape(block_rows, CW)
            g = acc[rows, cols] + jnp.dot(x, w2[end2, 0, :, cols], preferred_element_type=F32)
            u = acc[rows, more] + jnp.dot(x, w2[end2, 1, :, cols], preferred_element_type=F32)
            if both:
                x = x1[k1 - 1, zz].reshape(block_rows, CW)
                g = g + jnp.dot(x, w1[end1, 0, :, cols], preferred_element_type=F32)
                u = u + jnp.dot(x, w1[end1, 1, :, cols], preferred_element_type=F32)
            hid[rows, cols] = (g / (1.0 + jnp.exp(-g)) * u).astype(BF16)

    for i in range(2):
        done(w1.at[end1, i], w1_sem.at[end1, i])
        done(w2.at[end2, i], w2_sem.at[end2, i])
    for zz in (me.z, me.up, me.down):
        add_block(zz)
    done(x1.at[k1 - 1, across, low], f_recv.at[k1 - 1, 0])
    done(x1.at[k1 - 1, across, high], f_recv.at[k1 - 1, 1])
    done(x2.at[K2 - 1], a2_recv.at[K2 - 1])
    finish_block(across, True)
    load_down(w1, w1_sem, end1, end1)
    first_across(0)
    left_tokens(0)
    done(w2.at[0, 0], w2_sem.at[0, 0])
    other_block(across)
    first_across(1)
    for zz in (me.up, me.down):
        finish_block(zz)
    first_rest(0)
    finish_block(me.z)
    load_down(w2, w2_sem, end2, k1 + end2)
    for zz in (me.up, me.down, me.z):
        other_block(zz)
    refill_down(w2, w2_sem, 0, SLOTS2, K2, k1)
    first_rest(1)
    for k in range(2):
        down_block(y1.at[k], w1, k, me.z)
        refill_down(w1, w1_sem, k, SLOTS1, k1, 0)

    def third(k):
        done(s2.at[k, 0], s2_recv.at[k, 0])
        done(s2.at[k, 1], s2_recv.at[k, 1])
        left_plane(k)
        r1[k] = (y1[k, me.z].astype(F32) + s2[k, 0].astype(F32) + s2[k, 1].astype(F32)).astype(BF16)
        here = l1.at[k, me.j]
        for off in OFFS:
            j, device = me.plane(off)
            send(r1.at[k, j], here, b1_send.at[k], b1_recv.at[k], device)
        pltpu.make_async_copy(r1.at[k, me.j], here, b1_recv.at[k]).start()

    def combine(zz, rows):
        rows = rows.reshape(2 * PLANE * CAP, CW)
        return jnp.dot(gpk[zz, 0], rows, preferred_element_type=F32) + jnp.dot(
            gpk[zz, 1], rows, preferred_element_type=F32
        )

    def fourth(k):
        done(l1.at[k], b1_recv.at[k])
        t1[k] = combine(me.z, l1[k]).astype(BF16)
        send(t1.at[k, core_rows], e1.at[k], e1_send.at[k], e1_recv.at[k], me.core)

    def fifth(k):
        done(e1.at[k], e1_recv.at[k])
        out[:, pl.ds(pl.multiple_of(k * CW, CW), CW)] = plus(t1[k, own_rows], e1[k])

    def other_first(m):
        left_tokens(m)
        down(y2.at[m], w2, w2_sem, m, SLOTS2, K2, k1)
        here = l2.at[m, :, me.j]
        for off in OFFS:
            j, device = me.plane(off)
            send(y2.at[m, :, j], here, b2_send.at[m], b2_recv.at[m], device)
        pltpu.make_async_copy(y2.at[m, :, me.j], here, b2_recv.at[m]).start()

    def other_second(m):
        done(l2.at[m], b2_recv.at[m])

        @pl.loop(0, NZ)
        def _(zz):
            t2[zz, :, pl.ds(pl.multiple_of(m * CW, CW), CW)] = combine(zz, l2[m, zz]).astype(BF16)

        send(t2.at[:, core_rows, pl.ds(pl.multiple_of(m * CW, CW), CW)], e2.at[m], e2_send.at[m], e2_recv.at[m], me.core)

    def other_third(m):
        done(e2.at[m], e2_recv.at[m])
        for zz in range(NZ):
            u2[m, zz] = plus(t2[zz, own_rows, pl.ds(pl.multiple_of(m * CW, CW), CW)], e2[m, zz])
        send(u2.at[m, across, pl.ds(0, half)], v1.at[m, 0], v1_send.at[m, 0], v1_recv.at[m, 0], me.z_up)
        send(u2.at[m, across, pl.ds(half, half)], v1.at[m, 1], v1_send.at[m, 1], v1_recv.at[m, 1], me.z_down)

    def other_fourth(m):
        done(v1.at[m, 0], v1_recv.at[m, 0])
        u2[m, me.up, :half] = plus(u2[m, me.up, :half], v1[m, 0])
        send(u2.at[m, me.up], v2.at[m, 0], v2_send.at[m, 0], v2_recv.at[m, 0], me.z_up)
        done(v1.at[m, 1], v1_recv.at[m, 1])
        u2[m, me.down, half:] = plus(u2[m, me.down, half:], v1[m, 1])
        send(u2.at[m, me.down], v2.at[m, 1], v2_send.at[m, 1], v2_recv.at[m, 1], me.z_down)

    def other_fifth(m):
        done(v2.at[m, 0], v2_recv.at[m, 0])
        done(v2.at[m, 1], v2_recv.at[m, 1])
        total = u2[m, me.z].astype(F32) + v2[m, 0].astype(F32) + v2[m, 1].astype(F32)
        out[:, pl.ds(pl.multiple_of((k1 + m) * CW, CW), CW)] = total.astype(BF16)

    def in_pairs(k, lag, step):
        for i in range(2):
            @pl.when((k >= lag) & (2 * (k - lag) + i < k1))
            def _():
                step(2 * (k - lag) + i)

    @pl.loop(0, max(k1 + 6, 2 * K2 + 5))
    def _(k):
        between(k, 0, k1 - 2, lambda i: first(i + 2))
        between(k, 2, k1 - 2, lambda i: second(i + 2))
        between(k, 0, K2 - 1, lambda i: other_first(i + 1))
        between(k, 1, k1, third)
        n = k + 1
        for odd in range(2):
            @pl.when((n >= 3) & (n % 3 == odd) & (2 * (n // 3 - 1) + odd < K2))
            def _():
                other_second(2 * (n // 3 - 1) + odd)

        for at, step in ((k1 - 1, other_third), (k1, other_fourth)):
            @pl.when(k == at)
            def _():
                pl.loop(0, K2)(step)

        in_pairs(k, k1, fourth)

        @pl.when(k == k1 + 4)
        def _():
            pl.loop(0, K2)(other_fifth)

        in_pairs(k, k1 + 1, fifth)

    @pl.loop(0, k1)
    def _(k):
        for side in range(2):
            done(s1.at[k, 0], s1_send.at[k, side])
            done(s2.at[k, 0], s2_send.at[k, side])
        done(r1.at[k, pl.ds(0, PLANE - 1)], b1_send.at[k])
        done(e1.at[k], e1_send.at[k])

    @pl.loop(0, K2)
    def _(m):
        done(y2.at[m, :, pl.ds(0, PLANE - 1)], b2_send.at[m])
        done(e2.at[m], e2_send.at[m])
        for side in range(2):
            done(v1.at[m, 0], v1_send.at[m, side])
            done(v2.at[m, 0], v2_send.at[m, side])


def on_device(tokens, routes, gates, w_gate, w_up, w_down):
    width = tokens.shape[1]
    k1 = width // CW - K2
    hid_cols = w_gate.shape[2]
    rows = NZ * PLANE * 2 * CAP
    slots = 2 * CAP

    def dma(*shape):
        return pltpu.SemaphoreType.DMA(shape)

    vmem = pl.BlockSpec(memory_space=pltpu.VMEM)
    hbm = pl.BlockSpec(memory_space=pl.ANY)
    return pl.pallas_call(
        functools.partial(kernel, k1),
        out_shape=jax.ShapeDtypeStruct(tokens.shape, BF16),
        in_specs=[vmem, vmem, vmem, hbm, hbm, hbm],
        out_specs=vmem,
        scratch_shapes=[
            pltpu.VMEM((8, 2 * TOK), F32),
            pltpu.VMEM((NZ, 2, 8, 2 * TOK), F32),
            pltpu.VMEM((k1, 2 * TOK, CW), BF16),
            pltpu.VMEM((NZ, 2 * TOK, K2 * CW), BF16),
            pltpu.VMEM((NZ, PLANE * slots, 2 * TOK), BF16),
            pltpu.VMEM((NZ, 2, 2 * TOK, PLANE * slots), BF16),
            pltpu.VMEM((k1, PLANE, slots, CW), BF16),
            pltpu.VMEM((K2, NZ, PLANE, slots, CW), BF16),
            pltpu.VMEM((k1, NZ, PLANE, slots, CW), BF16),
            pltpu.VMEM((K2, NZ, PLANE, slots, CW), BF16),
            pltpu.VMEM((SLOTS1, 2, CW, hid_cols), BF16),
            pltpu.VMEM((SLOTS2, 2, CW, hid_cols), BF16),
            pltpu.VMEM((rows, 2 * hid_cols), F32),
            pltpu.VMEM((rows, hid_cols), BF16),
            pltpu.VMEM((k1, 2, PLANE // 2, slots, CW), BF16),
            pltpu.VMEM((k1, 2, PLANE, slots, CW), BF16),
            pltpu.VMEM((k1, PLANE, slots, CW), BF16),
            pltpu.VMEM((K2, NZ, PLANE, slots, CW), BF16),
            pltpu.VMEM((k1, TOK, CW), BF16),
            pltpu.VMEM((K2, NZ, TOK, CW), BF16),
            pltpu.VMEM((K2, NZ, TOK, CW), BF16),
            pltpu.VMEM((K2, 2, TOK // 2, CW), BF16),
            pltpu.VMEM((K2, 2, TOK, CW), BF16),
            dma(SLOTS1, 2), dma(SLOTS2, 2), dma(2 * NZ - 1), pltpu.SemaphoreType.DMA, dma(k1), dma(k1), dma(4), dma(5),
            pltpu.SemaphoreType.DMA, pltpu.SemaphoreType.DMA,
            dma(k1), dma(k1), dma(k1, 2), dma(k1, 2), dma(k1, 2), dma(k1, 2), dma(K2), dma(K2),
            dma(k1, 2), dma(k1, 2), dma(k1, 2), dma(k1, 2), dma(k1), dma(k1), dma(k1), dma(k1),
            dma(K2), dma(K2), dma(K2), dma(K2), dma(K2, 2), dma(K2, 2), dma(K2, 2), dma(K2, 2),
        ],
        compiler_params=pltpu.CompilerParams(collective_id=0, has_side_effects=True, vmem_limit_bytes=61 << 20),
    )(tokens, routes.T, gates.T, w_gate[0], w_up[0], w_down[0])


def solution(mesh):
    placed = (
        P(("rep", "head", "side"), None),
        P(("rep", "head", "side"), None),
        P(("rep", "head", "side"), None),
        P(("rep", "head"), None, "side"),
        P(("rep", "head"), None, "side"),
        P(("rep", "head"), "side", None),
    )
    return jax.shard_map(
        on_device,
        mesh=mesh,
        in_specs=placed,
        out_specs=P(("rep", "head", "side"), None),
        check_vma=False,
    )
```

```python
import functools

import jax
import jax.numpy as jnp
from jax import lax
from jax.experimental import pallas as pl
from jax.experimental.pallas import tpu as pltpu
from jax.sharding import PartitionSpec as P

MESH = pl.DeviceIdType.MESH
F32, BF16 = jnp.float32, jnp.bfloat16
CW = 512
K2 = 5
SLOTS1, SLOTS2 = 3, 3
CAP = 8
TOK = 64
NX, NY, NZ = 4, 4, 4
PLANE = NX * NY
OFFS = sorted(
    [(dx, dy) for dx in range(NX) for dy in range(NY) if (dx, dy) != (0, 0)],
    key=lambda off: min(off[0], NX - off[0]) + min(off[1], NY - off[1]),
)


class Place:
    def __init__(self):
        rep = lax.axis_index("rep")
        self.x, self.c = rep // 2, rep % 2
        self.y, self.z = lax.axis_index("head"), lax.axis_index("side")
        self.j = self.x * NY + self.y
        self.up, self.down = lax.rem(self.z + 1, NZ), lax.rem(self.z + NZ - 1, NZ)
        self.core = self.dev(self.x, 1 - self.c, self.y, self.z)
        self.z_up = self.dev(self.x, self.c, self.y, self.up)
        self.z_down = self.dev(self.x, self.c, self.y, self.down)

    def dev(self, x, c, y, z):
        return (x * 2 + c, y, z)

    def plane(self, off):
        x, y = lax.rem(self.x + off[0], NX), lax.rem(self.y + off[1], NY)
        return x * NY + y, self.dev(x, self.c, y, self.z)

    def column(self):
        own = []
        for dc in range(2):
            for dz in range(NZ):
                if (dc, dz) != (0, 0):
                    own.append(self.dev(self.x, lax.rem(self.c + dc, 2), self.y, lax.rem(self.z + dz, NZ)))
        return own


def greet(partners):
    for device in partners:
        pl.semaphore_signal(pltpu.get_barrier_semaphore(), inc=1, device_id=device, device_id_type=MESH)


def send(src, dst, send_sem, recv_sem, device):
    pltpu.make_async_remote_copy(
        src_ref=src, dst_ref=dst, send_sem=send_sem, recv_sem=recv_sem, device_id=device, device_id_type=MESH
    ).start()


def done(ref, sem):
    pltpu.make_async_copy(ref, ref, sem).wait()


def kernel(
    k1, tok, routes, gates, wg_hbm, wu_hbm, wd_hbm, out,
    meta, metas, tokc, ztok, pk, gpk, out1, out2, x1, x2, w1, w2, acc, hid,
    s1, s2, l1, l2, e1, e2, u2, v1, v2,
    w1_sem, w2_sem, m_send, m_recv, c_send, c_recv, t_send, t_recv, tc_send, tc_recv,
    a1_send, a1_recv, z_send, z_recv, f_send, f_recv, a2_send, a2_recv,
    s1_send, s1_recv, s2_send, s2_recv, b1_send, b1_recv, e1_send, e1_recv,
    b2_send, b2_recv, e2_send, e2_recv, v1_send, v1_recv, v2_send, v2_recv,
):
    y1, y2, r1, t1, t2 = x1, x2, out1, tokc, ztok
    me = Place()
    d1 = k1 * CW
    half = TOK // 2
    low, high = pl.ds(0, PLANE // 2), pl.ds(PLANE // 2, PLANE // 2)
    across = lax.rem(me.z + 2, NZ)
    own_rows = pl.ds(pl.multiple_of(me.c * TOK, TOK), TOK)
    core_rows = pl.ds(pl.multiple_of((1 - me.c) * TOK, TOK), TOK)

    def load_in(w, sem, slot, kk):
        rows = pl.ds(pl.multiple_of(kk * CW, CW), CW)
        pltpu.make_async_copy(wg_hbm.at[rows], w.at[slot, 0], sem.at[slot, 0]).start()
        pltpu.make_async_copy(wu_hbm.at[rows], w.at[slot, 1], sem.at[slot, 1]).start()

    def load_down(w, sem, slot, kk):
        cols = pl.ds(pl.multiple_of(kk * CW, CW), CW)
        pltpu.make_async_copy(wd_hbm.at[:, cols], w.at[slot, 0], sem.at[slot, 0]).start()

    partners = [me.plane(off)[1] for off in OFFS] + me.column()
    greet(partners)
    for k in range(SLOTS1):
        load_in(w1, w1_sem, k, k)
    for m in range(SLOTS2):
        load_in(w2, w2_sem, m, k1 + m)
    experts = 2 * PLANE
    expert = lax.broadcasted_iota(jnp.int32, (experts, TOK), 0)
    named = [jnp.where(expert == routes[i:i + 1, :], 1.0, 0.0) for i in range(2)]
    earlier = lax.broadcasted_iota(jnp.int32, (TOK, TOK), 0) < lax.broadcasted_iota(jnp.int32, (TOK, TOK), 1)
    before = jnp.dot((named[0] + named[1]).astype(BF16), jnp.where(earlier, 1.0, 0.0).astype(BF16), preferred_element_type=F32)
    parts = []
    for i in range(2):
        slot = jnp.sum(before * named[i], axis=0, keepdims=True)
        parts.append(routes[i:i + 1, :].astype(F32) * CAP + slot)
    parts += [gates[0:1, :], gates[1:2, :], jnp.zeros((4, TOK), F32)]
    own = jnp.concatenate(parts, axis=0)
    lane_core = lax.broadcasted_iota(jnp.int32, (8, 2 * TOK), 1) // TOK
    meta[...] = jnp.where(lane_core == me.c, jnp.concatenate([own, own], axis=1), 0.0)
    pl.semaphore_wait(pltpu.get_barrier_semaphore(), len(partners))

    own_meta = metas.at[me.z, me.c]
    pltpu.make_async_copy(meta, own_meta, m_recv).start()
    for i, device in enumerate(me.column()):
        send(meta, own_meta, m_send.at[i], m_recv, device)
    tail = pl.ds(d1, K2 * CW)
    own_tok = ztok.at[me.z, own_rows]
    send(tok.at[:, tail], own_tok, t_send.at[0], t_recv.at[0], me.z_up)
    send(tok.at[:, tail], own_tok, t_send.at[1], t_recv.at[1], me.z_down)
    for k in range(k1):
        cols = pl.ds(k * CW, CW)
        send(tok.at[:, cols], tokc.at[k, own_rows], c_send.at[k], c_recv.at[k], me.core)
        pltpu.make_async_copy(tok.at[:, cols], tokc.at[k, own_rows], c_recv.at[k]).start()
    pltpu.make_async_copy(tok.at[:, tail], own_tok, t_recv.at[4]).start()

    def hits(zz):
        shape = (2 * PLANE * CAP, 2 * TOK)
        row = lax.broadcasted_iota(jnp.int32, shape, 0)
        col = lax.broadcasted_iota(jnp.int32, shape, 1)
        dest = row // (2 * CAP)
        want = ((2 * (dest // NY) + me.c) * NY + dest % NY) * CAP + row % CAP
        want = jnp.where((row // CAP) % 2 == col // TOK, want, -1).astype(F32)
        both = metas[zz, 0] + metas[zz, 1]
        return both, want == both[0:1], want == both[1:2]

    def pickers(zz):
        _, hit0, hit1 = hits(zz)
        pk[zz] = jnp.where(hit0 | hit1, 1.0, 0.0).astype(BF16)

    def gated_pickers(zz):
        both, hit0, hit1 = hits(zz)
        gated = jnp.where(hit0, both[2:3], 0.0) + jnp.where(hit1, both[3:4], 0.0)
        gated = gated.T
        high = gated.astype(BF16)
        gpk[zz, 0] = high
        gpk[zz, 1] = (gated - high.astype(F32)).astype(BF16)

    done(metas, m_recv)
    pickers(me.z)

    def p1_issue(k):
        done(tokc.at[k], c_recv.at[k])
        picked = jnp.dot(pk[me.z], tokc[k], preferred_element_type=F32)
        out1[k] = picked.astype(BF16).reshape(PLANE, 2 * CAP, CW)
        here = x1.at[k, me.z, me.j]
        for off in OFFS:
            j, device = me.plane(off)
            send(out1.at[k, j], here, a1_send.at[k], a1_recv.at[k], device)
        pltpu.make_async_copy(out1.at[k, me.j], here, a1_recv.at[k]).start()

    def z_issue(k):
        block = x1.at[k, me.z]
        done(block, a1_recv.at[k])
        send(block, block, z_send.at[k, 0], z_recv.at[k, 0], me.z_up)
        send(block, block, z_send.at[k, 1], z_recv.at[k, 1], me.z_down)

    def z_forward(k):
        done(x1.at[k, me.down], z_recv.at[k, 0])
        part = x1.at[k, me.down, low]
        send(part, part, f_send.at[k, 0], f_recv.at[k, 0], me.z_up)
        done(x1.at[k, me.up], z_recv.at[k, 1])
        part = x1.at[k, me.up, high]
        send(part, part, f_send.at[k, 1], f_recv.at[k, 1], me.z_down)

    def project(block, w, sem, slot):
        hid_cols = hid.shape[1]
        for i in range(2):
            done(w.at[slot, i], sem.at[slot, i])

            @pl.loop(0, hid_cols // 256)
            def _(n):
                cols = pl.ds(pl.multiple_of(n * 256, 256), 256)
                to = pl.ds(pl.multiple_of(i * hid_cols + n * 256, 256), 256)
                part = jnp.dot(block[...].reshape(acc.shape[0], CW), w[slot, i, :, cols], preferred_element_type=F32)
                acc[:, to] = acc[:, to] + part

    def refill(w, sem, n, slots, count, base):
        slot = lax.rem(n, slots)

        @pl.when(n + slots < count)
        def _():
            load_in(w, sem, slot, base + n + slots)

        @pl.when(n + slots >= count)
        def _():
            load_down(w, sem, slot, base + slot)

    def mm1(k):
        done(x1.at[k, across, pl.ds(0, PLANE // 2)], f_recv.at[k, 0])
        done(x1.at[k, across, pl.ds(PLANE // 2, PLANE // 2)], f_recv.at[k, 1])
        project(x1.at[k], w1, w1_sem, lax.rem(k, SLOTS1))
        refill(w1, w1_sem, k, SLOTS1, k1, 0)

    def p2_issue(m):
        cols = pl.ds(pl.multiple_of(m * CW, CW), CW)

        @pl.loop(0, NZ)
        def _(zz):
            picked = jnp.dot(pk[zz], ztok[zz, :, cols], preferred_element_type=F32)
            out2[m, zz] = picked.astype(BF16).reshape(PLANE, 2 * CAP, CW)

        here = x2.at[m, :, me.j]
        for off in OFFS[::-1]:
            j, device = me.plane(off)
            send(out2.at[m, :, j], here, a2_send.at[m], a2_recv.at[m], device)
        pltpu.make_async_copy(out2.at[m, :, me.j], here, a2_recv.at[m]).start()

    def mm2(m):
        done(x2.at[m], a2_recv.at[m])
        project(x2.at[m], w2, w2_sem, lax.rem(m, SLOTS2))
        refill(w2, w2_sem, m, SLOTS2, K2, k1)

    p1_issue(0)
    p1_issue(1)
    done(ztok.at[me.down, own_rows], t_recv.at[0])
    part = ztok.at[me.down, pl.ds(pl.multiple_of(me.c * TOK, TOK), half)]
    send(part, part, t_send.at[2], t_recv.at[2], me.z_up)
    done(ztok.at[me.up, own_rows], t_recv.at[1])
    part = ztok.at[me.up, pl.ds(pl.multiple_of(me.c * TOK + half, half), half)]
    send(part, part, t_send.at[3], t_recv.at[3], me.z_down)
    z_issue(0)
    p1_issue(2)
    p1_issue(3)
    for dz in range(1, NZ):
        pickers(lax.rem(me.z + dz, NZ))
    z_issue(1)
    done(ztok.at[across, pl.ds(pl.multiple_of(me.c * TOK, TOK), half)], t_recv.at[2])
    done(ztok.at[across, pl.ds(pl.multiple_of(me.c * TOK + half, half), half)], t_recv.at[3])
    done(own_tok, t_recv.at[4])
    mine = ztok.at[:, own_rows]
    send(mine, mine, tc_send, tc_recv, me.core)
    acc[...] = jnp.zeros_like(acc)
    other = ztok.at[:, pl.ds(pl.multiple_of((1 - me.c) * TOK, TOK), TOK)]
    done(other, tc_recv)

    def between(k, lag, count, step):
        @pl.when((k >= lag) & (k < lag + count))
        def _():
            step(k - lag)

    def every_second(k, lag, step, count):
        @pl.when((k >= lag) & ((k - lag) % 2 == 0) & ((k - lag) // 2 < count))
        def _():
            step((k - lag) // 2)

    @pl.loop(0, max(k1 + 1, 3 + 2 * (K2 - 1)))
    def _(k):
        @pl.when((k >= 2) & (k < k1))
        def _():
            z_issue(k)

        between(k, 1, k1, z_forward)

        @pl.when(k + 4 < k1)
        def _():
            p1_issue(k + 4)

        every_second(k, 0, p2_issue, K2)
        between(k, 2, NZ, gated_pickers)
        between(k, 2, k1 - 1, mm1)
        every_second(k, 4, mm2, K2 - 1)

    for i in range(2 * NZ - 1):
        done(meta, m_send.at[i])
    done(tok.at[:, tail], t_send.at[0])
    done(tok.at[:, tail], t_send.at[1])
    done(ztok.at[0, pl.ds(0, half)], t_send.at[2])
    done(ztok.at[0, pl.ds(0, half)], t_send.at[3])
    done(mine, tc_send)

    def left_z(k):
        for side in range(2):
            done(x1.at[k, 0], z_send.at[k, side])
            done(x1.at[k, 0, low], f_send.at[k, side])

    def left_plane(k):
        done(tokc.at[k, pl.ds(0, TOK)], c_send.at[k])
        done(out1.at[k, pl.ds(0, PLANE - 1)], a1_send.at[k])

    def left_tokens(m):
        done(out2.at[m, :, pl.ds(0, PLANE - 1)], a2_send.at[m])

    def down_block(to, w, slot, zz):
        rows = pl.ds(pl.multiple_of(zz * PLANE * 2 * CAP, PLANE * 2 * CAP), PLANE * 2 * CAP)

        @pl.loop(0, CW // 256)
        def _(i):
            cols = pl.ds(pl.multiple_of(i * 256, 256), 256)
            part = jnp.dot(hid[rows, :], w[slot, 0, :, cols], preferred_element_type=F32)
            to[zz, :, :, cols] = part.astype(BF16).reshape(PLANE, 2 * CAP, 256)

    def down(to, w, sem, n, slots, count, base):
        slot = lax.rem(n, slots)
        done(w.at[slot, 0], sem.at[slot, 0])

        @pl.loop(0, CW // 256)
        def _(i):
            cols = pl.ds(pl.multiple_of(i * 256, 256), 256)
            part = jnp.dot(hid[...], w[slot, 0, :, cols], preferred_element_type=F32)
            to[:, :, :, cols] = part.astype(BF16).reshape(NZ, PLANE, 2 * CAP, 256)

        refill_down(w, sem, n, slots, count, base)

    def refill_down(w, sem, n, slots, count, base):
        @pl.when(n + slots < count)
        def _():
            load_down(w, sem, lax.rem(n, slots), base + n + slots)

    def plus(a, b):
        return (a.astype(F32) + b.astype(F32)).astype(BF16)

    def first_send(k):
        send(y1.at[k, across, low], s1.at[k, 0], s1_send.at[k, 0], s1_recv.at[k, 0], me.z_up)
        send(y1.at[k, across, high], s1.at[k, 1], s1_send.at[k, 1], s1_recv.at[k, 1], me.z_down)

    def first(k):
        left_z(k)
        down(y1.at[k], w1, w1_sem, k, SLOTS1, k1, 0)
        first_send(k)

    def second(k):
        done(s1.at[k, 0], s1_recv.at[k, 0])
        y1[k, me.up, low] = plus(y1[k, me.up, low], s1[k, 0])
        send(y1.at[k, me.up], s2.at[k, 0], s2_send.at[k, 0], s2_recv.at[k, 0], me.z_up)
        done(s1.at[k, 1], s1_recv.at[k, 1])
        y1[k, me.down, high] = plus(y1[k, me.down, high], s1[k, 1])
        send(y1.at[k, me.down], s2.at[k, 1], s2_send.at[k, 1], s2_recv.at[k, 1], me.z_down)

    def first_across(k):
        left_z(k)
        done(w1.at[k, 0], w1_sem.at[k, 0])
        down_block(y1.at[k], w1, k, across)
        first_send(k)

    def first_rest(k):
        for zz in (me.up, me.down):
            down_block(y1.at[k], w1, k, zz)
        second(k)

    def other_block(zz):
        down_block(y2.at[0], w2, 0, zz)
        here = l2.at[0, zz, me.j]
        for off in OFFS:
            j, device = me.plane(off)
            send(y2.at[0, zz, j], here, b2_send.at[0], b2_recv.at[0], device)
        pltpu.make_async_copy(y2.at[0, zz, me.j], here, b2_recv.at[0]).start()

    end1, end2 = (k1 - 1) % SLOTS1, (K2 - 1) % SLOTS2
    block_rows = PLANE * 2 * CAP

    def add_block(zz):
        rows = pl.ds(pl.multiple_of(zz * block_rows, block_rows), block_rows)
        for i in range(2):
            @pl.loop(0, hid.shape[1] // 256)
            def _(n):
                cols = pl.ds(pl.multiple_of(n * 256, 256), 256)
                to = pl.ds(pl.multiple_of(i * hid.shape[1] + n * 256, 256), 256)
                x = x1[k1 - 1, zz].reshape(block_rows, CW)
                acc[rows, to] = acc[rows, to] + jnp.dot(x, w1[end1, i, :, cols], preferred_element_type=F32)

    def finish_block(zz, both=False):
        rows = pl.ds(pl.multiple_of(zz * block_rows, block_rows), block_rows)

        @pl.loop(0, hid.shape[1] // 256)
        def _(n):
            cols = pl.ds(pl.multiple_of(n * 256, 256), 256)
            more = pl.ds(pl.multiple_of(hid.shape[1] + n * 256, 256), 256)
            x = x2[K2 - 1, zz].reshape(block_rows, CW)
            g = acc[rows, cols] + jnp.dot(x, w2[end2, 0, :, cols], preferred_element_type=F32)
            u = acc[rows, more] + jnp.dot(x, w2[end2, 1, :, cols], preferred_element_type=F32)
            if both:
                x = x1[k1 - 1, zz].reshape(block_rows, CW)
                g = g + jnp.dot(x, w1[end1, 0, :, cols], preferred_element_type=F32)
                u = u + jnp.dot(x, w1[end1, 1, :, cols], preferred_element_type=F32)
            hid[rows, cols] = (g / (1.0 + jnp.exp(-g)) * u).astype(BF16)

    for i in range(2):
        done(w1.at[end1, i], w1_sem.at[end1, i])
        done(w2.at[end2, i], w2_sem.at[end2, i])
    for zz in (me.z, me.up, me.down):
        add_block(zz)
    done(x1.at[k1 - 1, across, low], f_recv.at[k1 - 1, 0])
    done(x1.at[k1 - 1, across, high], f_recv.at[k1 - 1, 1])
    done(x2.at[K2 - 1], a2_recv.at[K2 - 1])
    finish_block(across, True)
    load_down(w1, w1_sem, end1, end1)
    first_across(0)
    left_tokens(0)
    done(w2.at[0, 0], w2_sem.at[0, 0])
    other_block(across)
    first_across(1)
    for zz in (me.up, me.down):
        finish_block(zz)
    first_rest(0)
    finish_block(me.z)
    load_down(w2, w2_sem, end2, k1 + end2)
    for zz in (me.up, me.down, me.z):
        other_block(zz)
    refill_down(w2, w2_sem, 0, SLOTS2, K2, k1)
    first_rest(1)
    for k in range(2):
        down_block(y1.at[k], w1, k, me.z)
        refill_down(w1, w1_sem, k, SLOTS1, k1, 0)

    def third(k):
        done(s2.at[k, 0], s2_recv.at[k, 0])
        done(s2.at[k, 1], s2_recv.at[k, 1])
        left_plane(k)
        r1[k] = (y1[k, me.z].astype(F32) + s2[k, 0].astype(F32) + s2[k, 1].astype(F32)).astype(BF16)
        here = l1.at[k, me.j]
        for off in OFFS:
            j, device = me.plane(off)
            send(r1.at[k, j], here, b1_send.at[k], b1_recv.at[k], device)
        pltpu.make_async_copy(r1.at[k, me.j], here, b1_recv.at[k]).start()

    def combine(zz, rows):
        rows = rows.reshape(2 * PLANE * CAP, CW)
        return jnp.dot(gpk[zz, 0], rows, preferred_element_type=F32) + jnp.dot(
            gpk[zz, 1], rows, preferred_element_type=F32
        )

    def fourth(k):
        done(l1.at[k], b1_recv.at[k])
        t1[k] = combine(me.z, l1[k]).astype(BF16)
        send(t1.at[k, core_rows], e1.at[k], e1_send.at[k], e1_recv.at[k], me.core)

    def fifth(k):
        done(e1.at[k], e1_recv.at[k])
        out[:, pl.ds(pl.multiple_of(k * CW, CW), CW)] = plus(t1[k, own_rows], e1[k])

    def other_first(m):
        left_tokens(m)
        down(y2.at[m], w2, w2_sem, m, SLOTS2, K2, k1)
        here = l2.at[m, :, me.j]
        for off in OFFS:
            j, device = me.plane(off)
            send(y2.at[m, :, j], here, b2_send.at[m], b2_recv.at[m], device)
        pltpu.make_async_copy(y2.at[m, :, me.j], here, b2_recv.at[m]).start()

    def other_second(m):
        done(l2.at[m], b2_recv.at[m])

        @pl.loop(0, NZ)
        def _(zz):
            t2[zz, :, pl.ds(pl.multiple_of(m * CW, CW), CW)] = combine(zz, l2[m, zz]).astype(BF16)

        send(t2.at[:, core_rows, pl.ds(pl.multiple_of(m * CW, CW), CW)], e2.at[m], e2_send.at[m], e2_recv.at[m], me.core)

    def other_third(m):
        done(e2.at[m], e2_recv.at[m])
        for zz in range(NZ):
            u2[m, zz] = plus(t2[zz, own_rows, pl.ds(pl.multiple_of(m * CW, CW), CW)], e2[m, zz])
        send(u2.at[m, across, pl.ds(0, half)], v1.at[m, 0], v1_send.at[m, 0], v1_recv.at[m, 0], me.z_up)
        send(u2.at[m, across, pl.ds(half, half)], v1.at[m, 1], v1_send.at[m, 1], v1_recv.at[m, 1], me.z_down)

    def other_fourth(m):
        done(v1.at[m, 0], v1_recv.at[m, 0])
        u2[m, me.up, :half] = plus(u2[m, me.up, :half], v1[m, 0])
        send(u2.at[m, me.up], v2.at[m, 0], v2_send.at[m, 0], v2_recv.at[m, 0], me.z_up)
        done(v1.at[m, 1], v1_recv.at[m, 1])
        u2[m, me.down, half:] = plus(u2[m, me.down, half:], v1[m, 1])
        send(u2.at[m, me.down], v2.at[m, 1], v2_send.at[m, 1], v2_recv.at[m, 1], me.z_down)

    def other_fifth(m):
        done(v2.at[m, 0], v2_recv.at[m, 0])
        done(v2.at[m, 1], v2_recv.at[m, 1])
        total = u2[m, me.z].astype(F32) + v2[m, 0].astype(F32) + v2[m, 1].astype(F32)
        out[:, pl.ds(pl.multiple_of((k1 + m) * CW, CW), CW)] = total.astype(BF16)

    def in_pairs(k, lag, step):
        for i in range(2):
            @pl.when((k >= lag) & (2 * (k - lag) + i < k1))
            def _():
                step(2 * (k - lag) + i)

    @pl.loop(0, max(k1 + 6, 2 * K2 + 5))
    def _(k):
        between(k, 0, k1 - 2, lambda i: first(i + 2))
        between(k, 2, k1 - 2, lambda i: second(i + 2))
        between(k, 0, K2 - 1, lambda i: other_first(i + 1))
        between(k, 1, k1, third)
        n = k + 1
        for odd in range(2):
            @pl.when((n >= 3) & (n % 3 == odd) & (2 * (n // 3 - 1) + odd < K2))
            def _():
                other_second(2 * (n // 3 - 1) + odd)

        for at, step in ((k1 - 1, other_third), (k1, other_fourth)):
            @pl.when(k == at)
            def _():
                pl.loop(0, K2)(step)

        in_pairs(k, k1, fourth)

        @pl.when(k == k1 + 4)
        def _():
            pl.loop(0, K2)(other_fifth)

        in_pairs(k, k1 + 1, fifth)

    @pl.loop(0, k1)
    def _(k):
        for side in range(2):
            done(s1.at[k, 0], s1_send.at[k, side])
            done(s2.at[k, 0], s2_send.at[k, side])
        done(r1.at[k, pl.ds(0, PLANE - 1)], b1_send.at[k])
        done(e1.at[k], e1_send.at[k])

    @pl.loop(0, K2)
    def _(m):
        done(y2.at[m, :, pl.ds(0, PLANE - 1)], b2_send.at[m])
        done(e2.at[m], e2_send.at[m])
        for side in range(2):
            done(v1.at[m, 0], v1_send.at[m, side])
            done(v2.at[m, 0], v2_send.at[m, side])


def hand_over(result, out, sem):
    copies = [
        pltpu.make_async_copy(result.at[pl.ds(i * 16, 16)], out.at[pl.ds(i * 16, 16)], sem.at[i]) for i in range(TOK // 16)
    ]
    for copy in copies:
        copy.start()
    for copy in copies:
        copy.wait()


def on_device(tokens, routes, gates, w_gate, w_up, w_down):
    width = tokens.shape[1]
    k1 = width // CW - K2
    hid_cols = w_gate.shape[2]
    rows = NZ * PLANE * 2 * CAP
    slots = 2 * CAP

    def dma(*shape):
        return pltpu.SemaphoreType.DMA(shape)

    vmem = pl.BlockSpec(memory_space=pltpu.VMEM)
    hbm = pl.BlockSpec(memory_space=pl.ANY)
    result = pl.pallas_call(
        functools.partial(kernel, k1),
        out_shape=jax.ShapeDtypeStruct(tokens.shape, BF16),
        in_specs=[vmem, vmem, vmem, hbm, hbm, hbm],
        out_specs=vmem,
        scratch_shapes=[
            pltpu.VMEM((8, 2 * TOK), F32),
            pltpu.VMEM((NZ, 2, 8, 2 * TOK), F32),
            pltpu.VMEM((k1, 2 * TOK, CW), BF16),
            pltpu.VMEM((NZ, 2 * TOK, K2 * CW), BF16),
            pltpu.VMEM((NZ, PLANE * slots, 2 * TOK), BF16),
            pltpu.VMEM((NZ, 2, 2 * TOK, PLANE * slots), BF16),
            pltpu.VMEM((k1, PLANE, slots, CW), BF16),
            pltpu.VMEM((K2, NZ, PLANE, slots, CW), BF16),
            pltpu.VMEM((k1, NZ, PLANE, slots, CW), BF16),
            pltpu.VMEM((K2, NZ, PLANE, slots, CW), BF16),
            pltpu.VMEM((SLOTS1, 2, CW, hid_cols), BF16),
            pltpu.VMEM((SLOTS2, 2, CW, hid_cols), BF16),
            pltpu.VMEM((rows, 2 * hid_cols), F32),
            pltpu.VMEM((rows, hid_cols), BF16),
            pltpu.VMEM((k1, 2, PLANE // 2, slots, CW), BF16),
            pltpu.VMEM((k1, 2, PLANE, slots, CW), BF16),
            pltpu.VMEM((k1, PLANE, slots, CW), BF16),
            pltpu.VMEM((K2, NZ, PLANE, slots, CW), BF16),
            pltpu.VMEM((k1, TOK, CW), BF16),
            pltpu.VMEM((K2, NZ, TOK, CW), BF16),
            pltpu.VMEM((K2, NZ, TOK, CW), BF16),
            pltpu.VMEM((K2, 2, TOK // 2, CW), BF16),
            pltpu.VMEM((K2, 2, TOK, CW), BF16),
            dma(SLOTS1, 2), dma(SLOTS2, 2), dma(2 * NZ - 1), pltpu.SemaphoreType.DMA, dma(k1), dma(k1), dma(4), dma(5),
            pltpu.SemaphoreType.DMA, pltpu.SemaphoreType.DMA,
            dma(k1), dma(k1), dma(k1, 2), dma(k1, 2), dma(k1, 2), dma(k1, 2), dma(K2), dma(K2),
            dma(k1, 2), dma(k1, 2), dma(k1, 2), dma(k1, 2), dma(k1), dma(k1), dma(k1), dma(k1),
            dma(K2), dma(K2), dma(K2), dma(K2), dma(K2, 2), dma(K2, 2), dma(K2, 2), dma(K2, 2),
        ],
        compiler_params=pltpu.CompilerParams(collective_id=0, has_side_effects=True, vmem_limit_bytes=61 << 20),
    )(tokens, routes.T, gates.T, w_gate[0], w_up[0], w_down[0])
    return pl.pallas_call(
        hand_over,
        out_shape=jax.ShapeDtypeStruct(tokens.shape, BF16),
        in_specs=[hbm],
        out_specs=hbm,
        scratch_shapes=[dma(4)],
    )(result)


def solution(mesh):
    placed = (
        P(("rep", "head", "side"), None),
        P(("rep", "head", "side"), None),
        P(("rep", "head", "side"), None),
        P(("rep", "head"), None, "side"),
        P(("rep", "head"), None, "side"),
        P(("rep", "head"), "side", None),
    )
    return jax.shard_map(
        on_device,
        mesh=mesh,
        in_specs=placed,
        out_specs=P(("rep", "head", "side"), None),
        check_vma=False,
    )
```
